512 devices in a mesh: seq: 32 (over z, y_hi, core), vocab: 16 (over y_lo, x).
Axes of the slice: x: 4, y: 8 (y_hi: 2, y_lo: 4; y = y_hi * 4 + y_lo), z: 8, core: 2. Of those that a mesh axis runs over, the one named last changes fastest.
Arguments:
- hidden: bfloat16 [4096, 4096], P('seq', 'vocab'), may hold values from -14 to 14
- head_weight: bfloat16 [2, 4096, 4096], P(None, None, 'vocab'), may hold values from -0.09375 to 0.09375
- gains: bfloat16 [2, 4096], P(None, 'vocab'), may hold values from 0.099609375 to 1.8984375
- unembed: bfloat16 [4096, 16384], P('seq', 'vocab'), may hold values from -3.5 to 3.5
- targets: int32 [2, 4096], P(None, 'seq'), may hold values from 0 to 16383
- loss_weights: float32 [2], replicated, may hold values from 2 to 8
Outputs:
- losses: float32 [2], replicated
- input_grad: float32 [4096, 4096], P('seq', 'vocab')
- gain_grad: float32 [2, 4096], P(None, 'vocab')
The draws below stay inside these ranges and needn't reach their ends.
All inputs are finite; a program needn't handle non-finite values.
Results may differ from the reference program's by a relative error of at most 0.02.
The reference program's roundings to bfloat16 on the way (of `normed`, `head_rows` and `upstream`) count: a program that leaves them out, or rounds other values in their place, can miss the bound.
Values may be sent and summed in bfloat16 or wider, within the bound.
A program may use at most 64 MiB of HBM per device.

```python
import math
import jax
import jax.numpy as jnp
import numpy as np
from jax import lax

D = 4096
VOC_DEV = 1024
HEADS = 2
VOCAB = 16384
TOKENS = 4096
N_VOCAB = 16


def draw_hidden(key, part):
    key = jax.random.fold_in(key, 11)
    base = jax.random.normal(key, (TOKENS, D), jnp.float32)
    return jnp.clip(base, -6.0, 6.0).astype(jnp.bfloat16)


def draw_unembed(key, part):
    key = jax.random.fold_in(key, 13)
    base = jax.random.normal(key, (D, VOCAB), jnp.float32) * 0.05
    return jnp.clip(base, -0.3, 0.3).astype(jnp.bfloat16)


def plant(entries, key, least, top_value):
    extent = entries.shape
    place = [jax.random.randint(jax.random.fold_in(key, axis), (), 0, extent[axis]) for axis in range(len(extent))]
    entries = entries.at[tuple(place)].set(least)
    longest = extent.index(max(extent))
    place[longest] = (place[longest] + 1) % extent[longest]
    return entries.at[tuple(place)].set(top_value)


def shard_levels(own_key, extent, split, smallest, high):
    factor_of, own = 1.0, jax.random.fold_in(own_key, 6)
    for axis_at, blocks in split:
        heights = jnp.exp(jax.random.uniform(jax.random.fold_in(own, axis_at), (blocks,), jnp.float32, smallest / len(split), high / len(split)))
        factor_of = factor_of * jnp.repeat(heights, extent[axis_at] // blocks).reshape([-1 if axis == axis_at else 1 for axis in range(len(extent))])
    return factor_of


def rank_bounds(amount, slope):
    weights = [(1 << 20) // math.isqrt(rank ** slope) + 1 for rank in range(1, amount + 1)]
    deviation = 1 + sum(weights) // (1 << 30)
    return np.cumsum(np.array([max(1, weight // deviation) for weight in weights]))


def ranked_ids(stream_key, shape, number_of, lean):
    grid = rank_bounds(number_of, lean)
    lot = jax.random.randint(jax.random.fold_in(stream_key, 1), shape, 0, int(grid[number_of - 1]))
    standing = jnp.searchsorted(jnp.asarray(grid, jnp.int32), lot, side="right")
    return jax.random.permutation(jax.random.fold_in(stream_key, 2), number_of)[standing].astype(jnp.int32)


def bell_draw(own_key, extent, spread, bound, shards=(), held_as=jnp.bfloat16):
    drawn = spread * jax.random.normal(own_key, extent, jnp.float32)
    if shards:
        drawn = drawn * shard_levels(own_key, extent, shards, -0.22, 0.18)
    return jnp.clip(drawn, -bound, bound).astype(held_as)


def setup_inputs(seed: int = 0) -> dict:
    splits = jax.random.split(jax.random.key(seed), 7)
    return {
        "hidden": draw_hidden(jax.random.fold_in(splits[6], 71), 0),
        "head_weight": bell_draw(splits[1], (HEADS, D, D), D ** -0.5, 0.09375, ((2, 16),)),
        "gains": jnp.clip(1.0 + 0.18 * jax.random.normal(splits[2], (HEADS, D), jnp.float32), 0.099609375, 1.8984375).astype(jnp.bfloat16),
        "unembed": draw_unembed(jax.random.fold_in(splits[6], 71), 0),
        "targets": plant(ranked_ids(splits[4], (HEADS, TOKENS), VOCAB, 2), jax.random.fold_in(splits[4], 3), 0, VOCAB - 1).astype(jnp.int32),
        "loss_weights": jnp.clip(jnp.exp(jax.random.uniform(splits[5], (HEADS,), jnp.float32, math.log(2.0), math.log(8.0))), 2.0, 8.0),
    }


eps = 1e-05

def block_product(left, right, block):

    def step(index, total):
        start = (index * block).astype(jnp.int32)
        left_part = lax.dynamic_slice_in_dim(left, start, block, 1)
        right_part = lax.dynamic_slice_in_dim(right, start, block, 1)
        partial_sum = lax.dot_general(left_part, right_part, (((1,), (1,)), ((), ())), preferred_element_type=jnp.float32)
        rounded = lax.optimization_barrier(partial_sum.astype(jnp.bfloat16))
        return total + rounded.astype(jnp.float32)
    empty = jnp.zeros((left.shape[0], right.shape[0]), jnp.float32)
    return lax.fori_loop(0, N_VOCAB, step, empty)

def reference(hidden, head_weight, gains, unembed, targets, loss_weights):
    x = hidden.astype(jnp.float32)
    r = lax.rsqrt(lax.optimization_barrier(jnp.mean(x * x, axis=-1, keepdims=True)) + eps)
    column_ids = lax.broadcasted_iota(jnp.int32, (1, VOCAB), 1)
    total_grad = jnp.zeros((TOKENS, D), jnp.float32)
    losses = []
    gain_grads = []
    for head in range(HEADS):
        gain_row = gains[head].astype(jnp.float32)[None, :]
        normed = (x * r * gain_row).astype(jnp.bfloat16)
        branch = jnp.dot(normed, head_weight[head], preferred_element_type=jnp.float32)
        head_rows = (x + branch).astype(jnp.bfloat16)
        logits = jnp.dot(head_rows, unembed, preferred_element_type=jnp.float32)
        top = lax.optimization_barrier(jnp.max(logits, axis=-1, keepdims=True))
        total = lax.optimization_barrier(jnp.sum(jnp.exp(logits - top), axis=-1, keepdims=True))
        lse = top + jnp.log(total)
        picked = column_ids == targets[head][:, None]
        target_logit = lax.optimization_barrier(jnp.sum(jnp.where(picked, logits, 0.0), axis=-1, keepdims=True))
        losses.append(jnp.sum(lse - target_logit) / TOKENS)
        upstream = (loss_weights[head] * (jnp.exp(logits - lse) - picked.astype(jnp.float32))).astype(jnp.bfloat16)
        head_grad = block_product(upstream, unembed, VOC_DEV)
        norm_grad = block_product(head_grad.astype(jnp.bfloat16), head_weight[head], D // N_VOCAB)
        scaled = gain_row * norm_grad
        dots = lax.optimization_barrier(jnp.sum(scaled * x, axis=-1, keepdims=True))
        input_part = r * scaled - x * r * r * r * dots / D
        total_grad = total_grad + head_grad + input_part
        gain_grads.append(lax.optimization_barrier(jnp.sum(norm_grad * x * r, axis=0)))
    return (jnp.stack(losses), total_grad, jnp.stack(gain_grads))
```

```python
import jax
import jax.numpy as jnp
from jax import lax
from jax.experimental import pallas as pl
from jax.experimental.pallas import tpu as pltpu
from jax.sharding import PartitionSpec as P

eps = 1e-05
NX, NY, NZ, NFAR, NCORE = 4, 4, 8, 2, 2
NV = NX * NY
PER_Z = NFAR * NCORE
MESH = pl.DeviceIdType.MESH
F32, BF16 = jnp.float32, jnp.bfloat16


def kernel(
    hidden, w_hbm, gains, unembed, targets, weights,
    grad_out, gain_out, loss_out,
    w, xg, hf, table, acc, up, low, tcol, rcol, lossrow,
    stat_x, stat_y, dot_x, dot_y, gain_p, gain_z,
    rs_send, rs_mid, rs_right, rs_left, rs_own, ys_send, ys_recv, head_grad, norm_grad,
    w_sem, xg_sem, hf_sem, far_sem, ring_sem, share_sem, stat_sem, dot_sem, gain_sem, rs_sem,
):
    rows, cols = hidden.shape
    heads = gains.shape[0]
    voc_dev = unembed.shape[1]
    width = cols * NV
    seq, voc = lax.axis_index("seq"), lax.axis_index("vocab")
    x, y = lax.rem(voc, NX), lax.div(voc, NX)
    z, far, core = lax.div(seq, PER_Z), lax.rem(lax.div(seq, NCORE), NFAR), lax.rem(seq, NCORE)
    right, left, over = lax.rem(x + 1, NX), lax.rem(x + 3, NX), lax.rem(x + 2, NX)

    def at_x(j):
        return (seq, y * NX + lax.rem(x + j, NX))

    def at_y(j):
        return (seq, lax.rem(y + j, NY) * NX + x)

    def at_z(j):
        return (lax.rem(z + j, NZ) * PER_Z + far * NCORE + core, voc)

    def at_pair(k):
        other_far = 1 - far if k // 2 else far
        other_core = 1 - core if k % 2 else core
        return (z * PER_Z + other_far * NCORE + other_core, voc)

    pending = []

    def send(src, dst, sems, k, to):
        copy = pltpu.make_async_remote_copy(
            src_ref=src, dst_ref=dst, send_sem=sems.at[0, k], recv_sem=sems.at[1, k],
            device_id=to, device_id_type=MESH,
        )
        copy.start()
        pending.append(copy)

    def arrive(dst, sems, k):
        pltpu.make_async_remote_copy(
            src_ref=dst, dst_ref=dst, send_sem=sems.at[0, k], recv_sem=sems.at[1, k],
            device_id=at_x(1), device_id_type=MESH,
        ).wait_recv()

    w_copy = pltpu.make_async_copy(w_hbm, w, w_sem)
    w_copy.start()
    barrier = pltpu.get_barrier_semaphore()
    partners = (
        [at_x(j) for j in range(1, NX)] + [at_y(j) for j in range(1, NY)]
        + [at_z(j) for j in range(1, NZ)] + [at_pair(k) for k in range(1, 4)]
    )
    for partner in partners:
        pl.semaphore_signal(barrier, inc=1, device_id=partner, device_id_type=MESH)
    xg[voc, 0:rows, :] = hidden[...]
    gain_rows = gains[...].astype(F32)
    gain_pad = jnp.concatenate(
        [jnp.broadcast_to(gain_rows[h : h + 1], (8, cols)) for h in range(heads)], axis=0
    )
    xg[voc, rows : rows + 8 * heads, :] = gain_pad.astype(BF16)
    table[pl.ds(pl.multiple_of(seq * rows, rows), rows), :] = unembed[...]
    pl.semaphore_wait(barrier, len(partners))

    def row(q):
        return lax.rem(y + NY - q, NY) * NX

    def gather_begin(buf, sems):
        for j in range(1, NY):
            send(buf.at[voc], buf.at[voc], sems, j - 1, at_y(j))
        send(buf.at[voc], buf.at[voc], sems, 3, at_x(1))
        send(buf.at[voc], buf.at[voc], sems, 7, at_x(NX - 1))

    def gather_row(buf, sems, q):
        slot = row(q) + x
        arrive(buf.at[slot], sems, q - 1)
        send(buf.at[slot], buf.at[slot], sems, 3 + q, at_x(1))
        send(buf.at[slot], buf.at[slot], sems, 7 + q, at_x(NX - 1))

    def gather_cross(buf, sems, q):
        if q < 2:
            slot, k, to = row(q) + left, 3 + q, at_x(1)
        else:
            slot, k, to = row(q) + right, 7 + q, at_x(NX - 1)
        arrive(buf.at[slot], sems, k)
        send(buf.at[slot], buf.at[slot], sems, 11 + q, to)

    def gather_end(buf, sems):
        for q in (2, 3):
            arrive(buf.at[row(q) + left], sems, 3 + q)
        for q in (0, 1):
            arrive(buf.at[row(q) + right], sems, 7 + q)
        for q in range(NY):
            arrive(buf.at[row(q) + over], sems, 11 + q)

    def slab(zz, e, own=True, first=0, count=rows):
        far_e = 1 - far if e else far
        core_e = core if own else 1 - core
        start = pl.multiple_of((zz * PER_Z + far_e * NCORE + core_e) * rows + first, count)
        return table.at[pl.ds(start, count), :]

    def z_at(j):
        return lax.rem(z + j + NZ, NZ)

    def share(e, k, zz):
        send(slab(zz, e), slab(zz, e), share_sem, e * NZ + k, at_pair(1))

    def ring_begin(e):
        if e:
            arrive(slab(z, 1), far_sem, 0)
        send(slab(z, e), slab(z, e), ring_sem, e * 8, at_z(1))
        send(slab(z, e), slab(z, e), ring_sem, e * 8 + 4, at_z(NZ - 1))
        share(e, 0, z)

    half = rows // 2

    def ring_step(e, h):
        for way, to in ((0, at_z(1)), (1, at_z(NZ - 1))):
            zz = z_at(h if way else -h)
            k = e * 8 + way * 4 + h
            arrive(slab(zz, e), ring_sem, k - 1)
            part = slab(zz, e) if h < 3 else slab(zz, e, True, way * half, half)
            send(part, part, ring_sem, k, to)
            share(e, 2 * h - 1 + way, zz)

    def ring_end(e):
        zz = z_at(4)
        for way in range(2):
            arrive(slab(zz, e, True, way * half, half), ring_sem, e * 8 + way * 4 + 3)
        share(e, 7, zz)

    def consume(e, first, last):
        far_e = 1 - far if e else far

        def body(k, carry):
            dist = lax.div(k + 1, 2)
            zz = lax.rem(z + NZ + dist * (1 - 2 * lax.rem(k, 2)), NZ)
            arrive(slab(zz, e, False), share_sem, e * NZ + k)
            block = zz * NFAR + far_e
            begin = pl.multiple_of(block * cols, cols)
            acc[...] += jnp.dot(hf[block], table[pl.ds(begin, cols), :], preferred_element_type=F32)
            return carry

        lax.fori_loop(first, last, body, 0)

    ring_begin(0)
    gather_begin(xg, xg_sem)
    send(slab(z, 0), slab(z, 0), far_sem, 0, at_pair(2))

    acc[...] = jnp.zeros_like(acc)
    for h in range(heads):
        t_row = targets[h : h + 1, :].astype(F32)
        tcol[h * rows : (h + 1) * rows, :] = jnp.broadcast_to(t_row, (rows, rows)).T
    own_x = hidden[...].astype(F32)

    for q in range(1, NY):
        gather_row(xg, xg_sem, q)
    ring_step(0, 1)
    for q in range(NY):
        gather_cross(xg, xg_sem, q)
    gather_end(xg, xg_sem)
    ring_step(0, 2)

    def square(k, total):
        block = xg[k, 0:rows, :].astype(F32)
        return total + block * block

    squares = lax.fori_loop(0, NV, square, jnp.zeros((rows, cols), F32))
    r = lax.rsqrt(jnp.sum(squares, axis=-1, keepdims=True) / width + eps)
    rcol[...] = jnp.broadcast_to(r, rcol.shape)
    w_copy.wait()

    def project(k, totals):
        scaled = xg[k, 0:rows, :].astype(F32) * rcol[:, 0:1]
        gain_k = xg[k, rows : rows + 8 * heads, :].astype(F32)
        begin = pl.multiple_of(k * cols, cols)
        out = []
        for h in range(heads):
            normed = (scaled * gain_k[8 * h : 8 * h + 1]).astype(BF16)
            out.append(
                totals[h]
                + jnp.dot(normed, w[h, pl.ds(begin, cols), :], preferred_element_type=F32)
            )
        return tuple(out)

    empty = jnp.zeros((rows, cols), F32)
    branches = lax.fori_loop(0, NV, project, (empty,) * heads)
    for h in range(heads):
        hf[voc, h * rows : (h + 1) * rows, :] = (own_x + branches[h]).astype(BF16)
    gather_begin(hf, hf_sem)
    ring_step(0, 3)
    ring_begin(1)
    for q in range(1, NY):
        gather_row(hf, hf_sem, q)
    ring_end(0)
    ring_step(1, 1)
    for q in range(NY):
        gather_cross(hf, hf_sem, q)
    ring_step(1, 2)
    gather_end(hf, hf_sem)

    consume(0, 0, NZ)
    ring_step(1, 3)
    consume(1, 0, 7)
    ring_end(1)
    consume(1, 7, NZ)

    col_ids = lax.broadcasted_iota(jnp.int32, (rows, voc_dev), 1) + voc * voc_dev
    lanes = lax.broadcasted_iota(jnp.int32, (rows, rows), 1)

    def picked(h):
        ids = tcol[h * rows : (h + 1) * rows, 0:1].astype(jnp.int32)
        return col_ids == ids

    def stat_rows(top, total, target):
        line = lax.broadcasted_iota(jnp.int32, (8, top.shape[1]), 0)
        return jnp.where(line == 0, top, jnp.where(line == 1, total, jnp.where(line == 2, target, 0.0)))

    def merge(slots, count):
        tops = [slots[j, 0:1, :] for j in range(count)]
        top = tops[0]
        for other in tops[1:]:
            top = jnp.maximum(top, other)
        total = jnp.zeros_like(top)
        target = jnp.zeros_like(top)
        for j in range(count):
            total = total + slots[j, 1:2, :] * jnp.exp(tops[j] - top)
            target = target + slots[j, 2:3, :]
        return top, total, target

    for h in range(heads):
        logits = acc[h * rows : (h + 1) * rows, :]
        top = jnp.max(logits, axis=-1, keepdims=True)
        total = jnp.sum(jnp.exp(logits - top), axis=-1, keepdims=True)
        target = jnp.sum(jnp.where(picked(h), logits, 0.0), axis=-1, keepdims=True)
        packed = jnp.where(lanes == 0, top, jnp.where(lanes == 1, total, jnp.where(lanes == 2, target, 0.0)))
        stat_x[0, :, h * rows : (h + 1) * rows] = packed.T[0:8, :]
    for j in range(1, NX):
        send(stat_x.at[0], stat_x.at[j], stat_sem, j - 1, at_x(j))
    for j in range(1, NX):
        arrive(stat_x.at[j], stat_sem, j - 1)
    stat_y[0] = stat_rows(*merge(stat_x, NX))
    for j in range(1, NY):
        send(stat_y.at[0], stat_y.at[j], stat_sem, 2 + j, at_y(j))
    for j in range(1, NY):
        arrive(stat_y.at[j], stat_sem, 2 + j)
    top, total, target = merge(stat_y, NY)
    lse = top + jnp.log(total)
    lossrow[...] = jnp.broadcast_to(lse - target, lossrow.shape)
    for h in range(heads):
        lse_col = jnp.broadcast_to(lse[:, h * rows : (h + 1) * rows], (rows, rows)).T[:, 0:1]
        probs = jnp.exp(acc[h * rows : (h + 1) * rows, :] - lse_col)
        upstream = weights[h] * (probs - jnp.where(picked(h), 1.0, 0.0))
        up[h] = upstream.T.astype(BF16)

    def partial(p, h, step, yb):
        block = yb * NX + lax.rem(x + step, NX)
        begin = pl.multiple_of(block * cols, cols)
        if p == 0:
            return jnp.dot(table[pl.ds(begin, cols), :], up[h], preferred_element_type=F32)
        return jnp.dot(w[h, pl.ds(begin, cols), :], low[h], preferred_element_type=F32)

    def reduce_across(p, h):
        i = p * heads + h

        def body(n, carry):
            rs_send[i, n] = partial(p, h, 2, n).astype(BF16)
            return carry

        lax.fori_loop(0, 4, body, 0)
        two, four = pl.ds(0, 2), pl.ds(2, 2)
        send(rs_send.at[i, two], rs_mid.at[i, two], rs_sem.at[i], 0, at_x(1))
        send(rs_send.at[i, four], rs_mid.at[i, four], rs_sem.at[i], 1, at_x(NX - 1))

    def reduce_near(p, h):
        i = p * heads + h

        def body(n, carry):
            g, b = lax.div(n, 2), lax.rem(n, 2)
            rs_send[i, 4 + n] = partial(p, h, 1 + 2 * g, 2 - 2 * g + b).astype(BF16)
            return carry

        lax.fori_loop(0, 4, body, 0)
        send(rs_send.at[i, pl.ds(4, 2)], rs_right.at[i, pl.ds(2, 2)], rs_sem.at[i], 2, at_x(1))
        send(rs_send.at[i, pl.ds(6, 2)], rs_left.at[i, pl.ds(0, 2)], rs_sem.at[i], 3, at_x(NX - 1))

    def reduce_own(p, h):
        i = p * heads + h

        def body(n, carry):
            rs_own[i, n] = partial(p, h, 0, n)
            return carry

        lax.fori_loop(0, 4, body, 0)

    def reduce_pass(p, h):
        i = p * heads + h
        arrive(rs_mid.at[i, pl.ds(0, 2)], rs_sem.at[i], 0)
        arrive(rs_mid.at[i, pl.ds(2, 2)], rs_sem.at[i], 1)

        def body(n, carry):
            g, b = lax.div(n, 2), lax.rem(n, 2)
            so_far = rs_mid[i, n].astype(F32)
            rs_send[i, 8 + n] = (partial(p, h, 1 + 2 * g, 2 * g + b) + so_far).astype(BF16)
            return carry

        lax.fori_loop(0, 4, body, 0)
        send(rs_send.at[i, pl.ds(8, 2)], rs_right.at[i, pl.ds(0, 2)], rs_sem.at[i], 4, at_x(1))
        send(rs_send.at[i, pl.ds(10, 2)], rs_left.at[i, pl.ds(2, 2)], rs_sem.at[i], 5, at_x(NX - 1))

    def reduce_column(p, h):
        i = p * heads + h
        arrive(rs_right.at[i, pl.ds(2, 2)], rs_sem.at[i], 2)
        arrive(rs_left.at[i, pl.ds(0, 2)], rs_sem.at[i], 3)
        arrive(rs_right.at[i, pl.ds(0, 2)], rs_sem.at[i], 4)
        arrive(rs_left.at[i, pl.ds(2, 2)], rs_sem.at[i], 5)
        for j in range(1, NY):
            yb = lax.rem(y + j, NY)
            total = rs_own[i, yb] + rs_right[i, yb].astype(F32) + rs_left[i, yb].astype(F32)
            ys_send[i, j - 1] = total.astype(BF16)
            send(ys_send.at[i, j - 1], ys_recv.at[i, j - 1], rs_sem.at[i], 5 + j, at_y(j))

    def reduce_end(p, h):
        i = p * heads + h
        total = rs_own[i, y] + rs_right[i, y].astype(F32) + rs_left[i, y].astype(F32)
        for j in range(1, NY):
            arrive(ys_recv.at[i, j - 1], rs_sem.at[i], 5 + j)
            total = total + ys_recv[i, j - 1].astype(F32)
        return total

    def head_done(h):
        total = reduce_end(0, h)
        low[h] = total.astype(BF16)
        head_grad[h] = total

    def norm_done(h):
        norm_grad[h] = reduce_end(1, h).T

    reduce_across(0, 0)
    reduce_near(0, 0)
    reduce_own(0, 0)
    reduce_pass(0, 0)
    reduce_across(0, 1)
    reduce_near(0, 1)
    reduce_column(0, 0)
    reduce_own(0, 1)
    reduce_pass(0, 1)
    head_done(0)
    reduce_across(1, 0)
    reduce_near(1, 0)
    reduce_own(1, 0)
    reduce_column(0, 1)
    reduce_pass(1, 0)
    head_done(1)
    reduce_across(1, 1)
    reduce_near(1, 1)
    reduce_own(1, 1)
    reduce_column(1, 0)
    reduce_pass(1, 1)
    norm_done(0)
    reduce_column(1, 1)
    norm_done(1)

    own_x = hidden[...].astype(F32)
    gain_rows = gains[...].astype(F32)
    r = rcol[:, 0:1]
    scaled = jnp.zeros((rows, cols), F32)
    for h in range(heads):
        scaled = scaled + gain_rows[h : h + 1] * norm_grad[h]
    dots = jnp.sum(scaled * own_x, axis=-1, keepdims=True)
    dot_x[0] = jnp.broadcast_to(dots, (rows, rows)).T[0:8, :]
    for j in range(1, NX):
        send(dot_x.at[0], dot_x.at[j], dot_sem, j - 1, at_x(j))
    line = lax.broadcasted_iota(jnp.int32, (8, cols), 0)
    packed = jnp.where(line == heads, lossrow[...], 0.0)
    for h in range(heads):
        part = jnp.sum(norm_grad[h] * own_x * r, axis=0, keepdims=True)
        packed = packed + jnp.where(line == h, part, 0.0)
    gain_p[0] = packed
    for k in range(1, 4):
        send(gain_p.at[0], gain_p.at[k], gain_sem, k - 1, at_pair(k))
    for j in range(1, NX):
        arrive(dot_x.at[j], dot_sem, j - 1)
    dot_y[0] = dot_x[0] + dot_x[1] + dot_x[2] + dot_x[3]
    for j in range(1, NY):
        send(dot_y.at[0], dot_y.at[j], dot_sem, 2 + j, at_y(j))
    for k in range(1, 4):
        arrive(gain_p.at[k], gain_sem, k - 1)
    gain_z[0] = gain_p[0] + gain_p[1] + gain_p[2] + gain_p[3]
    for j in range(1, NZ):
        send(gain_z.at[0], gain_z.at[j], gain_sem, 2 + j, at_z(j))
    for j in range(1, NY):
        arrive(dot_y.at[j], dot_sem, 2 + j)
    dots = dot_y[0] + dot_y[1] + dot_y[2] + dot_y[3]
    dot_col = jnp.broadcast_to(dots[0:1, :], (rows, rows)).T[:, 0:1]
    direct = (head_grad[0] + head_grad[1]).T
    grad_out[...] = direct + r * scaled - own_x * (r * r * r * dot_col / width)
    sums = gain_z[0]
    for j in range(1, NZ):
        arrive(gain_z.at[j], gain_sem, 2 + j)
        sums = sums + gain_z[j]
    gain_out[...] = sums[0:heads, :]
    spot = lax.broadcasted_iota(jnp.int32, loss_out.shape, 1)
    losses = jnp.zeros(loss_out.shape, F32)
    tokens = rows * NZ * PER_Z
    for h in range(heads):
        loss = jnp.sum(sums[heads : heads + 1, h * rows : (h + 1) * rows], axis=-1, keepdims=True)
        losses = losses + jnp.where(spot == h, loss / tokens, 0.0)
    loss_out[...] = losses
    for copy in pending:
        copy.wait_send()


def per_device(hidden, head_weight, gains, unembed, targets, loss_weights):
    rows, cols = hidden.shape
    heads = gains.shape[0]
    voc_dev = unembed.shape[1]
    both = heads * rows
    runs = 2 * heads
    vmem = pl.BlockSpec(memory_space=pltpu.VMEM)
    dma = pltpu.SemaphoreType.DMA
    grad, gain, loss = pl.pallas_call(
        kernel,
        out_shape=(
            jax.ShapeDtypeStruct((rows, cols), F32),
            jax.ShapeDtypeStruct((heads, cols), F32),
            jax.ShapeDtypeStruct((8, 128), F32),
        ),
        in_specs=[
            vmem,
            pl.BlockSpec(memory_space=pl.ANY),
            vmem,
            vmem,
            vmem,
            pl.BlockSpec(memory_space=pltpu.SMEM),
        ],
        out_specs=(vmem, vmem, vmem),
        scratch_shapes=[
            pltpu.VMEM(head_weight.shape, BF16),
            pltpu.VMEM((NV, rows + 8 * heads, cols), BF16),
            pltpu.VMEM((NV, both, cols), BF16),
            pltpu.VMEM((NV * cols, voc_dev), BF16),
            pltpu.VMEM((both, voc_dev), F32),
            pltpu.VMEM((heads, voc_dev, rows), BF16),
            pltpu.VMEM((heads, cols, rows), BF16),
            pltpu.VMEM((both, rows), F32),
            pltpu.VMEM((rows, rows), F32),
            pltpu.VMEM((8, both), F32),
            pltpu.VMEM((NX, 8, both), F32),
            pltpu.VMEM((NY, 8, both), F32),
            pltpu.VMEM((NX, 8, rows), F32),
            pltpu.VMEM((NY, 8, rows), F32),
            pltpu.VMEM((4, 8, cols), F32),
            pltpu.VMEM((NZ, 8, cols), F32),
            pltpu.VMEM((runs, 12, cols, rows), BF16),
            pltpu.VMEM((runs, 4, cols, rows), BF16),
            pltpu.VMEM((runs, 4, cols, rows), BF16),
            pltpu.VMEM((runs, 4, cols, rows), BF16),
            pltpu.VMEM((runs, 4, cols, rows), F32),
            pltpu.VMEM((runs, 3, cols, rows), BF16),
            pltpu.VMEM((runs, 3, cols, rows), BF16),
            pltpu.VMEM((heads, cols, rows), F32),
            pltpu.VMEM((heads, rows, cols), F32),
            dma,
            dma((2, 15)),
            dma((2, 15)),
            dma((2, 1)),
            dma((2, 16)),
            dma((2, 16)),
            dma((2, 6)),
            dma((2, 6)),
            dma((2, 10)),
            dma((runs, 2, 9)),
        ],
        compiler_params=pltpu.CompilerParams(
            collective_id=0, has_side_effects=True, vmem_limit_bytes=52 * 1024 * 1024
        ),
    )(hidden, head_weight, gains, unembed, targets, loss_weights)
    return loss[0, :heads], grad, gain


def solution(mesh):
    in_specs = (
        P("seq", "vocab"),
        P(None, None, "vocab"),
        P(None, "vocab"),
        P("seq", "vocab"),
        P(None, "seq"),
        P(),
    )
    out_specs = (P(), P("seq", "vocab"), P(None, "vocab"))
    return jax.shard_map(
        per_device, mesh=mesh, in_specs=in_specs, out_specs=out_specs, check_vma=False
    )
```

```python
import jax
import jax.numpy as jnp
from jax import lax
from jax.experimental import pallas as pl
from jax.experimental.pallas import tpu as pltpu
from jax.sharding import PartitionSpec as P

eps = 1e-05
NX, NY, NZ, NFAR, NCORE = 4, 4, 8, 2, 2
NV = NX * NY
PER_Z = NFAR * NCORE
MESH = pl.DeviceIdType.MESH
F32, BF16 = jnp.float32, jnp.bfloat16


def kernel(
    hidden_hbm, w_hbm, gains_hbm, unembed_hbm, targets_hbm, weights_hbm,
    grad_out, gain_out, loss_out,
    w, gains, targets, weights, xg, hf, normed, table, relay, acc, acc_t, up, low,
    x_t, gain_cols, rcol, r_line, lossrow, gain_rows,
    stat_x, stat_y, dot_x, dot_y, gain_p, gain_z,
    rs_send, rs_in, rs_part, rs_own, ys_send, ys_recv, head_grad, norm_grad,
    local_sem, xg_sem, hf_sem, far_sem, ring_sem, share_sem, stat_sem, dot_sem, gain_sem, rs_sem,
):
    rows, cols = hidden_hbm.shape
    heads = gains.shape[0]
    both = heads * rows
    voc_dev = unembed_hbm.shape[1]
    width = cols * NV
    seq, voc = lax.axis_index("seq"), lax.axis_index("vocab")
    x, y = lax.rem(voc, NX), lax.div(voc, NX)
    z, far, core = lax.div(seq, PER_Z), lax.rem(lax.div(seq, NCORE), NFAR), lax.rem(seq, NCORE)
    right, left, over = lax.rem(x + 1, NX), lax.rem(x + 3, NX), lax.rem(x + 2, NX)
    levels = NFAR * NY
    level = far * NY + y

    def at_x(j):
        return (seq, y * NX + lax.rem(x + j, NX))

    def at_y(j):
        return (seq, lax.rem(y + j, NY) * NX + x)

    def at_z(j):
        return (lax.rem(z + j, NZ) * PER_Z + far * NCORE + core, voc)

    def at_pair(k):
        other_far = 1 - far if k // 2 else far
        other_core = 1 - core if k % 2 else core
        return (z * PER_Z + other_far * NCORE + other_core, voc)

    def at_level(j):
        other = lax.rem(level + j + levels, levels)
        return (z * PER_Z + lax.div(other, NY) * NCORE + core, lax.rem(other, NY) * NX + x)

    pending = []

    def send(src, dst, sems, k, to):
        copy = pltpu.make_async_remote_copy(
            src_ref=src, dst_ref=dst, send_sem=sems.at[0, k], recv_sem=sems.at[1, k],
            device_id=to, device_id_type=MESH,
        )
        copy.start()
        pending.append(copy)

    def arrive(dst, sems, k):
        pltpu.make_async_remote_copy(
            src_ref=dst, dst_ref=dst, send_sem=sems.at[0, k], recv_sem=sems.at[1, k],
            device_id=at_x(1), device_id_type=MESH,
        ).wait_recv()

    own_rows = pl.ds(pl.multiple_of(seq * rows, rows), rows)
    fetches = [
        pltpu.make_async_copy(hidden_hbm, xg.at[voc, pl.ds(0, rows), :], local_sem.at[0]),
        pltpu.make_async_copy(unembed_hbm, table.at[own_rows, :], local_sem.at[1]),
        pltpu.make_async_copy(gains_hbm, gains, local_sem.at[2]),
        pltpu.make_async_copy(targets_hbm, targets, local_sem.at[3]),
        pltpu.make_async_copy(weights_hbm, weights, local_sem.at[4]),
        pltpu.make_async_copy(w_hbm, w, local_sem.at[5]),
    ]
    for fetch in fetches:
        fetch.start()
    barrier = pltpu.get_barrier_semaphore()
    partners = (
        [at_x(j) for j in range(1, NX)] + [at_y(j) for j in range(1, NY)]
        + [at_z(j) for j in range(1, NZ)] + [at_pair(k) for k in range(1, 4)]
        + [at_level(2), at_level(-2)]
    )
    for partner in partners:
        pl.semaphore_signal(barrier, inc=1, device_id=partner, device_id_type=MESH)
    for k in range(5):
        fetches[k].wait()
    gain_lines = gains[...].astype(F32)
    gain_pad = jnp.concatenate(
        [jnp.broadcast_to(gain_lines[h : h + 1], (8, cols)) for h in range(heads)], axis=0
    )
    xg[voc, rows : rows + 8 * heads, :] = gain_pad.astype(BF16)
    pl.semaphore_wait(barrier, len(partners))

    def row(q):
        return lax.rem(y + NY - q, NY) * NX

    def gather_begin(at, sems, base):
        for j in range(1, NY):
            send(at(voc), at(voc), sems, base + j - 1, at_y(j))
        send(at(voc), at(voc), sems, base + 3, at_x(1))
        send(at(voc), at(voc), sems, base + 7, at_x(NX - 1))

    def gather_row(at, sems, base, q):
        slot = row(q) + x
        arrive(at(slot), sems, base + q - 1)
        send(at(slot), at(slot), sems, base + 3 + q, at_x(1))
        send(at(slot), at(slot), sems, base + 7 + q, at_x(NX - 1))

    def gather_cross(at, sems, base, q):
        if q < 2:
            slot, k, to = row(q) + left, 3 + q, at_x(1)
        else:
            slot, k, to = row(q) + right, 7 + q, at_x(NX - 1)
        arrive(at(slot), sems, base + k)
        send(at(slot), at(slot), sems, base + 11 + q, to)

    def gather_end(at, sems, base):
        for q in (2, 3):
            arrive(at(row(q) + left), sems, base + 3 + q)
        for q in (0, 1):
            arrive(at(row(q) + right), sems, base + 7 + q)
        for q in range(NY):
            arrive(at(row(q) + over), sems, base + 11 + q)

    def x_at(slot):
        return xg.at[slot]

    def hf_at(h):
        return lambda slot: hf.at[slot, pl.ds(h * rows, rows), :]

    def slab(zz, e, own=True, first=0, count=rows):
        far_e = 1 - far if e else far
        core_e = core if own else 1 - core
        start = pl.multiple_of((zz * PER_Z + far_e * NCORE + core_e) * rows + first, count)
        return table.at[pl.ds(start, count), :]

    def z_at(j):
        return lax.rem(z + j + NZ, NZ)

    def share(e, k, zz):
        send(slab(zz, e), slab(zz, e), share_sem, e * NZ + k, at_pair(1))

    half = rows // 2

    def part_of(zz, e, p):
        return slab(zz, e, True, p * half, half)

    leg = 2 - 4 * core

    def far_begin():
        for p in range(2):
            send(part_of(z, 0, p), relay.at[p], far_sem, p, at_level(leg))

    def far_pass(p):
        arrive(relay.at[p], far_sem, p)
        source = lax.rem(level - leg + levels, levels)
        begin = (z * PER_Z + lax.div(source, NY) * NCORE + core) * rows + p * half
        place = table.at[pl.ds(pl.multiple_of(begin, half), half), :]
        send(relay.at[p], place, far_sem, 2 + p, at_level(leg))

    def ring_send(zz, e, way, h, p):
        block = part_of(zz, e, p)
        send(block, block, ring_sem, e * 14 + way * 7 + (h - 1) * 2 + (p if h < 4 else 0),
             at_z(NZ - 1 if way else 1))

    def ring_arrive(zz, e, way, h, p):
        arrive(part_of(zz, e, p), ring_sem, e * 14 + way * 7 + (h - 1) * 2 + (p if h < 4 else 0))

    def ring_begin(e, turn):
        if e:
            arrive(part_of(z, 1, turn), far_sem, 2 + turn)
        for way in range(2):
            ring_send(z, e, way, 1, turn if e else way ^ turn)
        if turn:
            share(e, 0, z)

    def ring_step(e, h, turn):
        for way in range(2):
            p = turn if e and h == 1 else way ^ turn
            zz = z_at(h if way else -h)
            ring_arrive(zz, e, way, h, p)
            if h < 3 or p == way:
                ring_send(zz, e, way, h + 1, p)
            if turn:
                share(e, 2 * h - 1 + way, zz)

    def ring_end(e):
        zz = z_at(4)
        for way in range(2):
            ring_arrive(zz, e, way, 4, way)
        share(e, 7, zz)

    def consume(e, first, last):
        far_e = 1 - far if e else far

        def body(k, carry):
            dist = lax.div(k + 1, 2)
            zz = lax.rem(z + NZ + dist * (1 - 2 * lax.rem(k, 2)), NZ)
            arrive(slab(zz, e, False), share_sem, e * NZ + k)
            block = zz * NFAR + far_e
            begin = pl.multiple_of(block * cols, cols)
            acc[...] += jnp.dot(hf[block], table[pl.ds(begin, cols), :], preferred_element_type=F32)
            return carry

        lax.fori_loop(first, last, body, 0)

    gather_begin(x_at, xg_sem, 0)
    ring_begin(0, 0)
    far_begin()
    ring_begin(0, 1)

    acc[...] = jnp.zeros_like(acc)
    own_x = xg[voc, 0:rows, :].astype(F32)
    x_t[...] = own_x.T
    for h in range(heads):
        gain_cols[h] = jnp.broadcast_to(gain_lines[h : h + 1], (rows, cols)).T

    for q in range(1, NY):
        gather_row(x_at, xg_sem, 0, q)
    ring_step(0, 1, 0)
    far_pass(0)
    gather_cross(x_at, xg_sem, 0, 0)
    gather_cross(x_at, xg_sem, 0, 2)
    ring_step(0, 1, 1)
    far_pass(1)
    gather_cross(x_at, xg_sem, 0, 1)
    gather_cross(x_at, xg_sem, 0, 3)
    ring_step(0, 2, 0)
    ring_begin(1, 0)
    ring_step(0, 2, 1)
    gather_end(x_at, xg_sem, 0)

    def square(k, total):
        block = xg[k, 0:rows, :].astype(F32)
        return total + block * block

    squares = lax.fori_loop(0, NV, square, jnp.zeros((rows, cols), F32))
    r = lax.rsqrt(jnp.sum(squares, axis=-1, keepdims=True) / width + eps)
    r_wide = jnp.broadcast_to(r, rcol.shape)
    rcol[...] = r_wide
    r_line[...] = r_wide.T[0:8, :]

    def norm(k, carry):
        scaled = xg[k, 0:rows, :].astype(F32) * rcol[:, 0:1]
        gain_k = xg[k, rows : rows + 8 * heads, :].astype(F32)
        begin = pl.multiple_of(k * cols, cols)
        for h in range(heads):
            normed[h, :, pl.ds(begin, cols)] = (scaled * gain_k[8 * h : 8 * h + 1]).astype(BF16)
        return carry

    ring_begin(1, 1)
    lax.fori_loop(0, NV, norm, 0)
    ring_step(0, 3, 0)
    fetches[5].wait()
    for h in range(heads):
        branch = jnp.dot(normed[h], w[h], preferred_element_type=F32)
        hf[voc, h * rows : (h + 1) * rows, :] = (own_x + branch).astype(BF16)
        gather_begin(hf_at(h), hf_sem, 15 * h)
        if h == 0:
            ring_step(1, 1, 0)
            ring_step(0, 3, 1)
    ring_step(1, 1, 1)
    for q in range(1, NY):
        gather_row(hf_at(0), hf_sem, 0, q)
    ring_end(0)
    ring_step(1, 2, 0)
    for q in range(1, NY):
        gather_row(hf_at(1), hf_sem, 15, q)
    for q in range(NY):
        gather_cross(hf_at(0), hf_sem, 0, q)
    ring_step(1, 2, 1)
    gather_cross(hf_at(1), hf_sem, 15, 0)
    gather_cross(hf_at(1), hf_sem, 15, 2)
    ring_step(1, 3, 0)
    gather_cross(hf_at(1), hf_sem, 15, 1)
    gather_cross(hf_at(1), hf_sem, 15, 3)
    gather_end(hf_at(0), hf_sem, 0)
    gather_end(hf_at(1), hf_sem, 15)

    consume(0, 0, 5)
    ring_step(1, 3, 1)
    consume(0, 5, NZ)
    consume(1, 0, 7)
    ring_end(1)
    consume(1, 7, NZ)

    step = 128
    ids = jnp.concatenate([targets[h : h + 1, :] for h in range(heads)], axis=1) - voc * voc_dev
    chunk_ids = lax.broadcasted_iota(jnp.int32, (step, both), 0)
    lane = lax.broadcasted_iota(jnp.int32, (1, both), 1)
    weight_row = jnp.full((1, both), weights[0], F32)
    for h in range(1, heads):
        weight_row = jnp.where(lane >= h * rows, weights[h], weight_row)

    def stat_rows(top, total, target):
        line = lax.broadcasted_iota(jnp.int32, (8, both), 0)
        return jnp.where(line == 0, top, jnp.where(line == 1, total, jnp.where(line == 2, target, 0.0)))

    def merge(slots, count):
        tops = [slots[j, 0:1, :] for j in range(count)]
        top = tops[0]
        for other in tops[1:]:
            top = jnp.maximum(top, other)
        total = jnp.zeros_like(top)
        target = jnp.zeros_like(top)
        for j in range(count):
            total = total + slots[j, 1:2, :] * jnp.exp(tops[j] - top)
            target = target + slots[j, 2:3, :]
        return top, total, target

    def turn(k, top):
        begin = pl.multiple_of(k * step, step)
        chunk = acc[:, pl.ds(begin, step)].T
        acc_t[pl.ds(begin, step), :] = chunk
        return jnp.maximum(top, jnp.max(chunk, axis=0, keepdims=True))

    first_chunk = acc[:, 0:step].T
    acc_t[0:step, :] = first_chunk
    top = lax.fori_loop(1, voc_dev // step, turn, jnp.max(first_chunk, axis=0, keepdims=True))

    def gauge(k, sums):
        begin = pl.multiple_of(k * step, step)
        chunk = acc_t[pl.ds(begin, step), :]
        total = jnp.sum(jnp.exp(chunk - top), axis=0, keepdims=True)
        hit = jnp.where(chunk_ids == ids - begin, chunk, 0.0)
        return sums[0] + total, sums[1] + jnp.sum(hit, axis=0, keepdims=True)

    empty = jnp.zeros((1, both), F32)
    total, target = lax.fori_loop(0, voc_dev // step, gauge, (empty, empty))
    stat_x[0] = stat_rows(top, total, target)
    for j in range(1, NX):
        send(stat_x.at[0], stat_x.at[j], stat_sem, j - 1, at_x(j))
    for j in range(1, NX):
        arrive(stat_x.at[j], stat_sem, j - 1)
    stat_y[0] = stat_rows(*merge(stat_x, NX))
    for j in range(1, NY):
        send(stat_y.at[0], stat_y.at[j], stat_sem, 2 + j, at_y(j))
    for j in range(1, NY):
        arrive(stat_y.at[j], stat_sem, 2 + j)
    top, total, target = merge(stat_y, NY)
    lse = top + jnp.log(total)
    lossrow[...] = jnp.broadcast_to(lse - target, lossrow.shape)

    def pull(k, carry):
        begin = pl.multiple_of(k * step, step)
        probs = jnp.exp(acc_t[pl.ds(begin, step), :] - lse)
        hit = jnp.where(chunk_ids == ids - begin, 1.0, 0.0)
        up[pl.ds(begin, step), :] = (weight_row * (probs - hit)).astype(BF16)
        return carry

    lax.fori_loop(0, voc_dev // step, pull, 0)

    def block_rows(way, yb):
        block = yb * NX + lax.rem(x + way, NX)
        return pl.ds(pl.multiple_of(block * cols, cols), cols)

    def head_part(way, yb):
        out = jnp.dot(table[block_rows(way, yb), :], up[...], preferred_element_type=F32)
        return [out[:, h * rows : (h + 1) * rows] for h in range(heads)]

    def norm_part(h, way, yb):
        return jnp.dot(w[h, block_rows(way, yb), :], low[h], preferred_element_type=F32)

    def across_of(n):
        way, b = lax.rem(n, 2), lax.div(n, 2)
        return way, 2 * way + b, 2 * way + b

    def near_of(n):
        way, b = lax.rem(n, 2), lax.div(n, 2)
        yb = 2 - 2 * way + b
        return way, yb, 4 + 4 * way + yb

    def last_of(n):
        way, b = lax.rem(n, 2), lax.div(n, 2)
        yb = 2 * way + b
        return way, yb, 4 + 4 * way + yb

    def loop4(body):
        def run(n, carry):
            body(n)
            return carry

        lax.fori_loop(0, 4, run, 0)

    def x_copy(i, way, slot):
        return pltpu.make_async_remote_copy(
            src_ref=rs_send.at[i, slot], dst_ref=rs_in.at[i, slot],
            send_sem=rs_sem.at[i, 0, slot], recv_sem=rs_sem.at[i, 1, slot],
            device_id=at_x(1 + 2 * way), device_id_type=MESH,
        )

    def x_arrive(i, slot):
        x_copy(i, 0, slot).wait_recv()

    def y_copy(i, yb):
        return pltpu.make_async_remote_copy(
            src_ref=ys_send.at[i, yb], dst_ref=ys_recv.at[i, y],
            send_sem=rs_sem.at[i, 0, 12 + yb], recv_sem=rs_sem.at[i, 1, 12 + y],
            device_id=(seq, yb * NX + x), device_id_type=MESH,
        )

    def y_arrive(i, yb):
        pltpu.make_async_remote_copy(
            src_ref=ys_send.at[i, yb], dst_ref=ys_recv.at[i, yb],
            send_sem=rs_sem.at[i, 0, 12 + yb], recv_sem=rs_sem.at[i, 1, 12 + yb],
            device_id=(seq, yb * NX + x), device_id_type=MESH,
        ).wait_recv()

    def column(i):
        for k in range(2):
            for yb in (k, k + 2):
                x_arrive(i, 4 + yb)
                x_arrive(i, 8 + yb)
                total = rs_own[i, yb] + rs_in[i, 4 + yb].astype(F32) + rs_in[i, 8 + yb].astype(F32)
                rs_own[i, yb] = total
                ys_send[i, yb] = total.astype(BF16)

                @pl.when(y != yb)
                def _():
                    y_copy(i, yb).start()

    def finish(i):
        total = rs_own[i, y]
        for j in range(1, NY):
            peer = lax.rem(y + j, NY)
            y_arrive(i, peer)
            total = total + ys_recv[i, peer].astype(F32)
        return total

    def across_heads(n):
        way, yb, slot = across_of(n)
        for h, part in enumerate(head_part(2, yb)):
            rs_send[h, slot] = part.astype(BF16)
        x_copy(0, way, slot).start()

    def near_heads(n):
        way, yb, slot = near_of(n)
        for h, part in enumerate(head_part(1 + 2 * way, yb)):
            rs_send[h, slot] = part.astype(BF16)
        x_copy(0, way, slot).start()

    def last_heads(n):
        way, yb, slot = last_of(n)
        for h, part in enumerate(head_part(1 + 2 * way, yb)):
            rs_part[h, yb] = part

    def own_heads(n):
        for h, part in enumerate(head_part(0, n)):
            rs_own[h, n] = part

    def send_heads(h):
        def across(n):
            way, yb, slot = across_of(n)
            x_copy(h, way, slot).start()

        def near(n):
            way, yb, slot = near_of(n)
            x_copy(h, way, slot).start()

        loop4(across)
        loop4(near)

    def pass_heads(h):
        def body(n):
            way, yb, slot = last_of(n)
            x_arrive(h, yb)
            rs_send[h, slot] = (rs_part[h, yb] + rs_in[h, yb].astype(F32)).astype(BF16)
            x_copy(h, way, slot).start()

        loop4(body)

    def head_done(h):
        total = finish(h)
        low[h] = total.astype(BF16)
        head_grad[h] = total

    def norm_begin(h):
        i = heads + h

        def across(n):
            way, yb, slot = across_of(n)
            rs_send[i, slot] = norm_part(h, 2, yb).astype(BF16)
            x_copy(i, way, slot).start()

        def near(n):
            way, yb, slot = near_of(n)
            rs_send[i, slot] = norm_part(h, 1 + 2 * way, yb).astype(BF16)
            x_copy(i, way, slot).start()

        loop4(across)
        loop4(near)

    def norm_pass(h):
        i = heads + h

        def own(n):
            rs_own[i, n] = norm_part(h, 0, n)

        def last(n):
            way, yb, slot = last_of(n)
            part = norm_part(h, 1 + 2 * way, yb)
            x_arrive(i, yb)
            rs_send[i, slot] = (part + rs_in[i, yb].astype(F32)).astype(BF16)
            x_copy(i, way, slot).start()

        loop4(own)
        loop4(last)

    def norm_done(h):
        norm_grad[h] = finish(heads + h)

    def gain_done(h):
        weighed = norm_grad[h] * x_t[...] * r_line[0:1, :]
        part = jnp.sum(weighed.T, axis=0, keepdims=True)
        gain_rows[8 * h : 8 * h + 8, :] = jnp.broadcast_to(part, (8, cols))

    loop4(across_heads)
    loop4(near_heads)
    loop4(last_heads)
    pass_heads(0)
    send_heads(1)
    loop4(own_heads)
    column(0)
    pass_heads(1)
    head_done(0)
    norm_begin(0)
    column(1)
    norm_pass(0)
    head_done(1)
    norm_begin(1)
    column(2)
    norm_pass(1)
    norm_done(0)
    gain_done(0)
    column(3)
    norm_done(1)

    scaled = jnp.zeros((cols, rows), F32)
    for h in range(heads):
        scaled = scaled + gain_cols[h] * norm_grad[h]
    dots = jnp.sum(scaled * x_t[...], axis=0, keepdims=True)
    dot_x[0] = jnp.broadcast_to(dots, (8, rows))
    for j in range(1, NX):
        send(dot_x.at[0], dot_x.at[j], dot_sem, j - 1, at_x(j))
    for h in range(1, heads):
        gain_done(h)
    line = lax.broadcasted_iota(jnp.int32, (8, cols), 0)
    packed = jnp.where(line == heads, lossrow[...], 0.0)
    for h in range(heads):
        packed = packed + jnp.where(line == h, gain_rows[8 * h : 8 * h + 8, :], 0.0)
    gain_p[0] = packed
    for k in range(1, 4):
        send(gain_p.at[0], gain_p.at[k], gain_sem, k - 1, at_pair(k))
    for j in range(1, NX):
        arrive(dot_x.at[j], dot_sem, j - 1)
    dot_y[0] = dot_x[0] + dot_x[1] + dot_x[2] + dot_x[3]
    for j in range(1, NY):
        send(dot_y.at[0], dot_y.at[j], dot_sem, 2 + j, at_y(j))
    r_row = r_line[0:1, :]
    direct = (head_grad[0] + head_grad[1] + r_row * scaled).T
    for k in range(1, 4):
        arrive(gain_p.at[k], gain_sem, k - 1)
    gain_z[0] = gain_p[0] + gain_p[1] + gain_p[2] + gain_p[3]
    for j in range(1, NZ):
        send(gain_z.at[0], gain_z.at[j], gain_sem, 2 + j, at_z(j))
    for j in range(1, NY):
        arrive(dot_y.at[j], dot_sem, 2 + j)
    dots = dot_y[0] + dot_y[1] + dot_y[2] + dot_y[3]
    back = r_row * r_row * r_row * dots[0:1, :] / width
    back_col = jnp.broadcast_to(back, (rows, rows)).T[:, 0:1]
    grad_out[...] = direct - xg[voc, 0:rows, :].astype(F32) * back_col
    sums = gain_z[0]
    for j in range(1, NZ):
        arrive(gain_z.at[j], gain_sem, 2 + j)
        sums = sums + gain_z[j]
    gain_out[...] = sums[0:heads, :]
    spot = lax.broadcasted_iota(jnp.int32, loss_out.shape, 1)
    losses = jnp.zeros(loss_out.shape, F32)
    tokens = rows * NZ * PER_Z
    for h in range(heads):
        loss = jnp.sum(sums[heads : heads + 1, h * rows : (h + 1) * rows], axis=-1, keepdims=True)
        losses = losses + jnp.where(spot == h, loss / tokens, 0.0)
    loss_out[...] = losses
    for copy in pending:
        copy.wait_send()
    for i in range(2 * heads):
        for slot in range(12):
            x_copy(i, 0, slot).wait_send()
        for j in range(1, NY):
            y_copy(i, lax.rem(y + j, NY)).wait_send()


def per_device(hidden, head_weight, gains, unembed, targets, loss_weights):
    rows, cols = hidden.shape
    heads = gains.shape[0]
    voc_dev = unembed.shape[1]
    both = heads * rows
    runs = 2 * heads
    vmem = pl.BlockSpec(memory_space=pltpu.VMEM)
    dma = pltpu.SemaphoreType.DMA
    grad, gain, loss = pl.pallas_call(
        kernel,
        out_shape=(
            jax.ShapeDtypeStruct((rows, cols), F32),
            jax.ShapeDtypeStruct((heads, cols), F32),
            jax.ShapeDtypeStruct((8, 128), F32),
        ),
        in_specs=[pl.BlockSpec(memory_space=pltpu.HBM)] * 6,
        out_specs=(vmem, vmem, vmem),
        scratch_shapes=[
            pltpu.VMEM(head_weight.shape, BF16),
            pltpu.VMEM(gains.shape, BF16),
            pltpu.VMEM(targets.shape, jnp.int32),
            pltpu.SMEM(loss_weights.shape, F32),
            pltpu.VMEM((NV, rows + 8 * heads, cols), BF16),
            pltpu.VMEM((NV, both, cols), BF16),
            pltpu.VMEM((heads, rows, NV * cols), BF16),
            pltpu.VMEM((NV * cols, voc_dev), BF16),
            pltpu.VMEM((2, rows // 2, voc_dev), BF16),
            pltpu.VMEM((both, voc_dev), F32),
            pltpu.VMEM((voc_dev, both), F32),
            pltpu.VMEM((voc_dev, both), BF16),
            pltpu.VMEM((heads, cols, rows), BF16),
            pltpu.VMEM((cols, rows), F32),
            pltpu.VMEM((heads, cols, rows), F32),
            pltpu.VMEM((rows, rows), F32),
            pltpu.VMEM((8, rows), F32),
            pltpu.VMEM((8, both), F32),
            pltpu.VMEM((8 * heads, cols), F32),
            pltpu.VMEM((NX, 8, both), F32),
            pltpu.VMEM((NY, 8, both), F32),
            pltpu.VMEM((NX, 8, rows), F32),
            pltpu.VMEM((NY, 8, rows), F32),
            pltpu.VMEM((4, 8, cols), F32),
            pltpu.VMEM((NZ, 8, cols), F32),
            pltpu.VMEM((runs, 12, cols, rows), BF16),
            pltpu.VMEM((runs, 12, cols, rows), BF16),
            pltpu.VMEM((heads, 4, cols, rows), F32),
            pltpu.VMEM((runs, 4, cols, rows), F32),
            pltpu.VMEM((runs, 4, cols, rows), BF16),
            pltpu.VMEM((runs, 4, cols, rows), BF16),
            pltpu.VMEM((heads, cols, rows), F32),
            pltpu.VMEM((heads, cols, rows), F32),
            dma((6,)),
            dma((2, 15)),
            dma((2, 15 * heads)),
            dma((2, 4)),
            dma((2, 28)),
            dma((2, 16)),
            dma((2, 6)),
            dma((2, 6)),
            dma((2, 10)),
            dma((runs, 2, 16)),
        ],
        compiler_params=pltpu.CompilerParams(
            collective_id=0, has_side_effects=True, vmem_limit_bytes=60 * 1024 * 1024
        ),
    )(hidden, head_weight, gains, unembed, targets, loss_weights)
    return loss[0, :heads], grad, gain


def solution(mesh):
    in_specs = (
        P("seq", "vocab"),
        P(None, None, "vocab"),
        P(None, "vocab"),
        P("seq", "vocab"),
        P(None, "seq"),
        P(),
    )
    out_specs = (P(), P("seq", "vocab"), P(None, "vocab"))
    return jax.shard_map(
        per_device, mesh=mesh, in_specs=in_specs, out_specs=out_specs, check_vma=False
    )
```

```python
import jax
import jax.numpy as jnp
from jax import lax
from jax.experimental import pallas as pl
from jax.experimental.pallas import tpu as pltpu
from jax.sharding import PartitionSpec as P

eps = 1e-05
NX, NY, NZ, NFAR, NCORE = 4, 4, 8, 2, 2
NV = NX * NY
PER_Z = NFAR * NCORE
MESH = pl.DeviceIdType.MESH
F32, BF16 = jnp.float32, jnp.bfloat16


def kernel(
    hidden_hbm, w_hbm, gains_hbm, unembed_hbm, targets_hbm, weights_hbm,
    grad_out, gain_out, loss_out,
    w, gains, targets, weights, xg, hf, normed, table, relay, acc, acc_t, up, low,
    x_t, gain_cols, rcol, r_line, lossrow, gain_rows,
    stat_x, stat_y, dot_x, dot_y, gain_p, gain_z,
    rs_send, rs_in, rs_part, rs_own, ys_send, ys_recv, head_grad, norm_grad,
    local_sem, xg_sem, hf_sem, far_sem, ring_sem, share_sem, stat_sem, dot_sem, gain_sem, rs_sem,
):
    rows, cols = hidden_hbm.shape
    heads = gains.shape[0]
    both = heads * rows
    voc_dev = unembed_hbm.shape[1]
    width = cols * NV
    seq, voc = lax.axis_index("seq"), lax.axis_index("vocab")
    x, y = lax.rem(voc, NX), lax.div(voc, NX)
    z, far, core = lax.div(seq, PER_Z), lax.rem(lax.div(seq, NCORE), NFAR), lax.rem(seq, NCORE)
    right, left, over = lax.rem(x + 1, NX), lax.rem(x + 3, NX), lax.rem(x + 2, NX)
    levels = NFAR * NY
    level = far * NY + y

    def at_x(j):
        return (seq, y * NX + lax.rem(x + j, NX))

    def at_y(j):
        return (seq, lax.rem(y + j, NY) * NX + x)

    def at_z(j):
        return (lax.rem(z + j, NZ) * PER_Z + far * NCORE + core, voc)

    def at_pair(k):
        other_far = 1 - far if k // 2 else far
        other_core = 1 - core if k % 2 else core
        return (z * PER_Z + other_far * NCORE + other_core, voc)

    def at_level(j):
        other = lax.rem(level + j + levels, levels)
        return (z * PER_Z + lax.div(other, NY) * NCORE + core, lax.rem(other, NY) * NX + x)

    pending = []

    def send(src, dst, sems, k, to):
        copy = pltpu.make_async_remote_copy(
            src_ref=src, dst_ref=dst, send_sem=sems.at[0, k], recv_sem=sems.at[1, k],
            device_id=to, device_id_type=MESH,
        )
        copy.start()
        pending.append(copy)

    def arrive(dst, sems, k):
        pltpu.make_async_remote_copy(
            src_ref=dst, dst_ref=dst, send_sem=sems.at[0, k], recv_sem=sems.at[1, k],
            device_id=at_x(1), device_id_type=MESH,
        ).wait_recv()

    own_rows = pl.ds(pl.multiple_of(seq * rows, rows), rows)
    fetches = [
        pltpu.make_async_copy(hidden_hbm, xg.at[voc, pl.ds(0, rows), :], local_sem.at[0]),
        pltpu.make_async_copy(unembed_hbm, table.at[own_rows, :], local_sem.at[1]),
        pltpu.make_async_copy(gains_hbm, gains, local_sem.at[2]),
        pltpu.make_async_copy(targets_hbm, targets, local_sem.at[3]),
        pltpu.make_async_copy(weights_hbm, weights, local_sem.at[4]),
        pltpu.make_async_copy(w_hbm, w, local_sem.at[5]),
    ]
    for fetch in fetches:
        fetch.start()
    barrier = pltpu.get_barrier_semaphore()
    partners = (
        [at_x(j) for j in range(1, NX)] + [at_y(j) for j in range(1, NY)]
        + [at_z(j) for j in range(1, NZ)] + [at_pair(k) for k in range(1, 4)]
        + [at_level(2), at_level(-2)]
    )
    for partner in partners:
        pl.semaphore_signal(barrier, inc=1, device_id=partner, device_id_type=MESH)
    for k in range(5):
        fetches[k].wait()
    gain_lines = gains[...].astype(F32)
    gain_pad = jnp.concatenate(
        [jnp.broadcast_to(gain_lines[h : h + 1], (8, cols)) for h in range(heads)], axis=0
    )
    xg[voc, rows : rows + 8 * heads, :] = gain_pad.astype(BF16)
    pl.semaphore_wait(barrier, len(partners))

    def row(q):
        return lax.rem(y + NY - q, NY) * NX

    def gather_begin(at, sems, base):
        for j in range(1, NY):
            send(at(voc), at(voc), sems, base + j - 1, at_y(j))
        send(at(voc), at(voc), sems, base + 3, at_x(1))
        send(at(voc), at(voc), sems, base + 7, at_x(NX - 1))

    def gather_row(at, sems, base, q):
        slot = row(q) + x
        arrive(at(slot), sems, base + q - 1)
        send(at(slot), at(slot), sems, base + 3 + q, at_x(1))
        send(at(slot), at(slot), sems, base + 7 + q, at_x(NX - 1))

    def gather_cross(at, sems, base, q):
        if q < 2:
            slot, k, to = row(q) + left, 3 + q, at_x(1)
        else:
            slot, k, to = row(q) + right, 7 + q, at_x(NX - 1)
        arrive(at(slot), sems, base + k)
        send(at(slot), at(slot), sems, base + 11 + q, to)

    def gather_end(at, sems, base):
        for q in (2, 3):
            arrive(at(row(q) + left), sems, base + 3 + q)
        for q in (0, 1):
            arrive(at(row(q) + right), sems, base + 7 + q)
        for q in range(NY):
            arrive(at(row(q) + over), sems, base + 11 + q)

    half = rows // 2
    pads = 8 * heads

    def x_at(t):
        return lambda slot: xg.at[slot, pl.ds(t * half, half + t * pads), :]

    def hf_at(t):
        return lambda slot: hf.at[slot, pl.ds(t * rows, rows), :]

    def slab(zz, e, own=True, first=0, count=rows):
        far_e = 1 - far if e else far
        core_e = core if own else 1 - core
        start = pl.multiple_of((zz * PER_Z + far_e * NCORE + core_e) * rows + first, count)
        return table.at[pl.ds(start, count), :]

    def z_at(j):
        return lax.rem(z + j + NZ, NZ)

    def share(e, k, zz):
        send(slab(zz, e), slab(zz, e), share_sem, e * NZ + k, at_pair(1))

    def part_of(zz, e, p):
        return slab(zz, e, True, p * half, half)

    leg = 2 - 4 * core

    def far_begin():
        for p in range(2):
            send(part_of(z, 0, p), relay.at[p], far_sem, p, at_level(leg))

    def far_pass(p):
        arrive(relay.at[p], far_sem, p)
        source = lax.rem(level - leg + levels, levels)
        begin = (z * PER_Z + lax.div(source, NY) * NCORE + core) * rows + p * half
        place = table.at[pl.ds(pl.multiple_of(begin, half), half), :]
        send(relay.at[p], place, far_sem, 2 + p, at_level(leg))

    def ring_send(zz, e, way, h, p):
        block = part_of(zz, e, p)
        send(block, block, ring_sem, e * 14 + way * 7 + (h - 1) * 2 + (p if h < 4 else 0),
             at_z(NZ - 1 if way else 1))

    def ring_arrive(zz, e, way, h, p):
        arrive(part_of(zz, e, p), ring_sem, e * 14 + way * 7 + (h - 1) * 2 + (p if h < 4 else 0))

    def ring_begin(e, turn):
        if e:
            arrive(part_of(z, 1, turn), far_sem, 2 + turn)
        for way in range(2):
            ring_send(z, e, way, 1, turn if e else way ^ turn)
        if turn:
            share(e, 0, z)

    def ring_step(e, h, turn):
        for way in range(2):
            p = turn if e and h == 1 else way ^ turn
            zz = z_at(h if way else -h)
            ring_arrive(zz, e, way, h, p)
            if h < 3 or p == way:
                ring_send(zz, e, way, h + 1, p)
            if turn:
                share(e, 2 * h - 1 + way, zz)

    def ring_end(e):
        zz = z_at(4)
        for way in range(2):
            ring_arrive(zz, e, way, 4, way)
        share(e, 7, zz)

    def consume(e, first, last):
        far_e = 1 - far if e else far

        def body(k, carry):
            dist = lax.div(k + 1, 2)
            zz = lax.rem(z + NZ + dist * (1 - 2 * lax.rem(k, 2)), NZ)
            arrive(slab(zz, e, False), share_sem, e * NZ + k)
            block = zz * NFAR + far_e
            begin = pl.multiple_of(block * cols, cols)
            lines = [
                hf[block, t * rows + h * half : t * rows + (h + 1) * half, :]
                for h in range(heads) for t in range(2)
            ]
            acc[...] += jnp.dot(
                jnp.concatenate(lines, axis=0), table[pl.ds(begin, cols), :],
                preferred_element_type=F32,
            )
            return carry

        lax.fori_loop(first, last, body, 0)

    for t in (1, 0):
        gather_begin(x_at(t), xg_sem, 15 * t)
    ring_begin(0, 0)
    ring_begin(0, 1)

    acc[...] = jnp.zeros_like(acc)
    own_x = xg[voc, 0:rows, :].astype(F32)
    x_t[...] = own_x.T
    for h in range(heads):
        gain_cols[h] = jnp.broadcast_to(gain_lines[h : h + 1], (rows, cols)).T

    def project(t):
        lo = t * half

        def square(k, total):
            block = xg[k, lo : lo + half, :].astype(F32)
            return total + block * block

        squares = lax.fori_loop(0, NV, square, jnp.zeros((half, cols), F32))
        r = lax.rsqrt(jnp.sum(squares, axis=-1, keepdims=True) / width + eps)
        rcol[lo : lo + half, :] = jnp.broadcast_to(r, (half, rows))

        def norm(k, carry):
            scaled = xg[k, lo : lo + half, :].astype(F32) * rcol[lo : lo + half, 0:1]
            begin = pl.multiple_of(k * cols, cols)
            gain_k = xg[k, rows : rows + pads, :].astype(F32)
            for h in range(heads):
                line = (scaled * gain_k[8 * h : 8 * h + 1]).astype(BF16)
                normed[h, lo : lo + half, pl.ds(begin, cols)] = line
            return carry

        lax.fori_loop(0, NV, norm, 0)
        for h in range(heads):
            branch = jnp.dot(normed[h, lo : lo + half, :], w[h], preferred_element_type=F32)
            total = xg[voc, lo : lo + half, :].astype(F32) + branch
            at = t * rows + h * half
            hf[voc, at : at + half, :] = total.astype(BF16)
        gather_begin(hf_at(t), hf_sem, 15 * t)

    for q in range(1, NY):
        gather_row(x_at(1), xg_sem, 15, q)
    far_begin()
    ring_step(0, 1, 0)
    for q in range(1, NY):
        gather_row(x_at(0), xg_sem, 0, q)
    for q in (0, 2, 1, 3):
        gather_cross(x_at(1), xg_sem, 15, q)
    ring_step(0, 1, 1)
    far_pass(0)
    for q in (0, 2, 1, 3):
        gather_cross(x_at(0), xg_sem, 0, q)
    gather_end(x_at(1), xg_sem, 15)
    ring_step(0, 2, 0)
    far_pass(1)
    fetches[5].wait()
    project(1)
    ring_step(0, 2, 1)
    gather_end(x_at(0), xg_sem, 0)
    ring_begin(1, 0)
    ring_step(0, 3, 0)
    project(0)
    r_line[...] = rcol[...].T[0:8, :]
    ring_begin(1, 1)
    ring_step(0, 3, 1)
    for q in range(1, NY):
        gather_row(hf_at(1), hf_sem, 15, q)
    ring_step(1, 1, 0)
    for q in (0, 2, 1, 3):
        gather_cross(hf_at(1), hf_sem, 15, q)
    ring_end(0)
    for q in range(1, NY):
        gather_row(hf_at(0), hf_sem, 0, q)
    ring_step(1, 1, 1)
    for q in (0, 2, 1, 3):
        gather_cross(hf_at(0), hf_sem, 0, q)
    ring_step(1, 2, 0)
    gather_end(hf_at(1), hf_sem, 15)
    gather_end(hf_at(0), hf_sem, 0)

    consume(0, 0, 3)
    ring_step(1, 2, 1)
    consume(0, 3, 6)
    ring_step(1, 3, 0)
    consume(0, 6, NZ)
    consume(1, 0, 3)
    ring_step(1, 3, 1)
    consume(1, 3, 7)
    ring_end(1)
    consume(1, 7, NZ)

    step = 128
    ids = jnp.concatenate([targets[h : h + 1, :] for h in range(heads)], axis=1) - voc * voc_dev
    chunk_ids = lax.broadcasted_iota(jnp.int32, (step, both), 0)
    lane = lax.broadcasted_iota(jnp.int32, (1, both), 1)
    weight_row = jnp.full((1, both), weights[0], F32)
    for h in range(1, heads):
        weight_row = jnp.where(lane >= h * rows, weights[h], weight_row)

    def stat_rows(top, total, target):
        line = lax.broadcasted_iota(jnp.int32, (8, both), 0)
        return jnp.where(line == 0, top, jnp.where(line == 1, total, jnp.where(line == 2, target, 0.0)))

    def merge(slots, count):
        tops = [slots[j, 0:1, :] for j in range(count)]
        top = tops[0]
        for other in tops[1:]:
            top = jnp.maximum(top, other)
        total = jnp.zeros_like(top)
        target = jnp.zeros_like(top)
        for j in range(count):
            total = total + slots[j, 1:2, :] * jnp.exp(tops[j] - top)
            target = target + slots[j, 2:3, :]
        return top, total, target

    def turn(k, top):
        begin = pl.multiple_of(k * step, step)
        chunk = acc[:, pl.ds(begin, step)].T
        acc_t[pl.ds(begin, step), :] = chunk
        return jnp.maximum(top, jnp.max(chunk, axis=0, keepdims=True))

    first_chunk = acc[:, 0:step].T
    acc_t[0:step, :] = first_chunk
    top = lax.fori_loop(1, voc_dev // step, turn, jnp.max(first_chunk, axis=0, keepdims=True))

    def gauge(k, sums):
        begin = pl.multiple_of(k * step, step)
        chunk = acc_t[pl.ds(begin, step), :]
        total = jnp.sum(jnp.exp(chunk - top), axis=0, keepdims=True)
        hit = jnp.where(chunk_ids == ids - begin, chunk, 0.0)
        return sums[0] + total, sums[1] + jnp.sum(hit, axis=0, keepdims=True)

    empty = jnp.zeros((1, both), F32)
    total, target = lax.fori_loop(0, voc_dev // step, gauge, (empty, empty))
    stat_x[0] = stat_rows(top, total, target)
    for j in range(1, NX):
        send(stat_x.at[0], stat_x.at[j], stat_sem, j - 1, at_x(j))
    for j in range(1, NX):
        arrive(stat_x.at[j], stat_sem, j - 1)
    stat_y[0] = stat_rows(*merge(stat_x, NX))
    for j in range(1, NY):
        send(stat_y.at[0], stat_y.at[j], stat_sem, 2 + j, at_y(j))
    for j in range(1, NY):
        arrive(stat_y.at[j], stat_sem, 2 + j)
    top, total, target = merge(stat_y, NY)
    lse = top + jnp.log(total)
    lossrow[...] = jnp.broadcast_to(lse - target, lossrow.shape)

    def pull(k, carry):
        begin = pl.multiple_of(k * step, step)
        probs = jnp.exp(acc_t[pl.ds(begin, step), :] - lse)
        hit = jnp.where(chunk_ids == ids - begin, 1.0, 0.0)
        up[pl.ds(begin, step), :] = (weight_row * (probs - hit)).astype(BF16)
        return carry

    lax.fori_loop(0, voc_dev // step, pull, 0)

    def block_rows(way, yb):
        block = yb * NX + lax.rem(x + way, NX)
        return pl.ds(pl.multiple_of(block * cols, cols), cols)

    def head_part(way, yb):
        out = jnp.dot(table[block_rows(way, yb), :], up[...], preferred_element_type=F32)
        return [out[:, h * rows : (h + 1) * rows] for h in range(heads)]

    def norm_part(h, way, yb):
        return jnp.dot(w[h, block_rows(way, yb), :], low[h], preferred_element_type=F32)

    def across_of(n):
        way, b = lax.rem(n, 2), lax.div(n, 2)
        return way, 2 * way + b, 2 * way + b

    def near_of(n):
        way, b = lax.rem(n, 2), lax.div(n, 2)
        yb = 2 - 2 * way + b
        return way, yb, 4 + 4 * way + yb

    def last_of(n):
        way, b = lax.rem(n, 2), lax.div(n, 2)
        yb = 2 * way + b
        return way, yb, 4 + 4 * way + yb

    def loop4(body):
        def run(n, carry):
            body(n)
            return carry

        lax.fori_loop(0, 4, run, 0)

    def x_copy(i, way, slot):
        return pltpu.make_async_remote_copy(
            src_ref=rs_send.at[i, slot], dst_ref=rs_in.at[i, slot],
            send_sem=rs_sem.at[i, 0, slot], recv_sem=rs_sem.at[i, 1, slot],
            device_id=at_x(1 + 2 * way), device_id_type=MESH,
        )

    def x_arrive(i, slot):
        x_copy(i, 0, slot).wait_recv()

    def y_copy(i, yb):
        return pltpu.make_async_remote_copy(
            src_ref=ys_send.at[i, yb], dst_ref=ys_recv.at[i, y],
            send_sem=rs_sem.at[i, 0, 12 + yb], recv_sem=rs_sem.at[i, 1, 12 + y],
            device_id=(seq, yb * NX + x), device_id_type=MESH,
        )

    def y_arrive(i, yb):
        pltpu.make_async_remote_copy(
            src_ref=ys_send.at[i, yb], dst_ref=ys_recv.at[i, yb],
            send_sem=rs_sem.at[i, 0, 12 + yb], recv_sem=rs_sem.at[i, 1, 12 + yb],
            device_id=(seq, yb * NX + x), device_id_type=MESH,
        ).wait_recv()

    def column(i):
        for k in range(2):
            for yb in (k, k + 2):
                x_arrive(i, 4 + yb)
                x_arrive(i, 8 + yb)
                total = rs_own[i, yb] + rs_in[i, 4 + yb].astype(F32) + rs_in[i, 8 + yb].astype(F32)
                rs_own[i, yb] = total
                ys_send[i, yb] = total.astype(BF16)

                @pl.when(y != yb)
                def _():
                    y_copy(i, yb).start()

    def finish(i):
        total = rs_own[i, y]
        for j in range(1, NY):
            peer = lax.rem(y + j, NY)
            y_arrive(i, peer)
            total = total + ys_recv[i, peer].astype(F32)
        return total

    def across_heads(n):
        way, yb, slot = across_of(n)
        for h, part in enumerate(head_part(2, yb)):
            rs_send[h, slot] = part.astype(BF16)
        x_copy(0, way, slot).start()

    def near_heads(n):
        way, yb, slot = near_of(n)
        for h, part in enumerate(head_part(1 + 2 * way, yb)):
            rs_send[h, slot] = part.astype(BF16)
        x_copy(0, way, slot).start()

    def last_heads(n):
        way, yb, slot = last_of(n)
        for h, part in enumerate(head_part(1 + 2 * way, yb)):
            rs_part[h, yb] = part

    def own_heads(n):
        for h, part in enumerate(head_part(0, n)):
            rs_own[h, n] = part

    def send_heads(h):
        def across(n):
            way, yb, slot = across_of(n)
            x_copy(h, way, slot).start()

        def near(n):
            way, yb, slot = near_of(n)
            x_copy(h, way, slot).start()

        loop4(across)
        loop4(near)

    def pass_heads(h):
        def body(n):
            way, yb, slot = last_of(n)
            x_arrive(h, yb)
            rs_send[h, slot] = (rs_part[h, yb] + rs_in[h, yb].astype(F32)).astype(BF16)
            x_copy(h, way, slot).start()

        loop4(body)

    def head_done(h):
        total = finish(h)
        low[h] = total.astype(BF16)
        head_grad[h] = total

    def norm_begin(h):
        i = heads + h

        def across(n):
            way, yb, slot = across_of(n)
            rs_send[i, slot] = norm_part(h, 2, yb).astype(BF16)
            x_copy(i, way, slot).start()

        def near(n):
            way, yb, slot = near_of(n)
            rs_send[i, slot] = norm_part(h, 1 + 2 * way, yb).astype(BF16)
            x_copy(i, way, slot).start()

        loop4(across)
        loop4(near)

    def norm_pass(h):
        i = heads + h

        def own(n):
            rs_own[i, n] = norm_part(h, 0, n)

        def last(n):
            way, yb, slot = last_of(n)
            part = norm_part(h, 1 + 2 * way, yb)
            x_arrive(i, yb)
            rs_send[i, slot] = (part + rs_in[i, yb].astype(F32)).astype(BF16)
            x_copy(i, way, slot).start()

        loop4(own)
        loop4(last)

    def norm_done(h):
        norm_grad[h] = finish(heads + h)

    def gain_done(h):
        weighed = norm_grad[h] * x_t[...] * r_line[0:1, :]
        part = jnp.sum(weighed.T, axis=0, keepdims=True)
        gain_rows[8 * h : 8 * h + 8, :] = jnp.broadcast_to(part, (8, cols))

    loop4(across_heads)
    loop4(near_heads)
    loop4(last_heads)
    pass_heads(0)
    send_heads(1)
    loop4(own_heads)
    column(0)
    pass_heads(1)
    head_done(0)
    norm_begin(0)
    column(1)
    norm_pass(0)
    head_done(1)
    norm_begin(1)
    column(2)
    norm_pass(1)
    norm_done(0)
    gain_done(0)
    column(3)
    norm_done(1)

    scaled = jnp.zeros((cols, rows), F32)
    for h in range(heads):
        scaled = scaled + gain_cols[h] * norm_grad[h]
    dots = jnp.sum(scaled * x_t[...], axis=0, keepdims=True)
    dot_x[0] = jnp.broadcast_to(dots, (8, rows))
    for j in range(1, NX):
        send(dot_x.at[0], dot_x.at[j], dot_sem, j - 1, at_x(j))
    for h in range(1, heads):
        gain_done(h)
    line = lax.broadcasted_iota(jnp.int32, (8, cols), 0)
    packed = jnp.where(line == heads, lossrow[...], 0.0)
    for h in range(heads):
        packed = packed + jnp.where(line == h, gain_rows[8 * h : 8 * h + 8, :], 0.0)
    gain_p[0] = packed
    for k in range(1, 4):
        send(gain_p.at[0], gain_p.at[k], gain_sem, k - 1, at_pair(k))
    for j in range(1, NX):
        arrive(dot_x.at[j], dot_sem, j - 1)
    dot_y[0] = dot_x[0] + dot_x[1] + dot_x[2] + dot_x[3]
    for j in range(1, NY):
        send(dot_y.at[0], dot_y.at[j], dot_sem, 2 + j, at_y(j))
    r_row = r_line[0:1, :]
    direct = (head_grad[0] + head_grad[1] + r_row * scaled).T
    for k in range(1, 4):
        arrive(gain_p.at[k], gain_sem, k - 1)
    gain_z[0] = gain_p[0] + gain_p[1] + gain_p[2] + gain_p[3]
    for j in range(1, NZ):
        send(gain_z.at[0], gain_z.at[j], gain_sem, 2 + j, at_z(j))
    for j in range(1, NY):
        arrive(dot_y.at[j], dot_sem, 2 + j)
    dots = dot_y[0] + dot_y[1] + dot_y[2] + dot_y[3]
    back = r_row * r_row * r_row * dots[0:1, :] / width
    back_col = jnp.broadcast_to(back, (rows, rows)).T[:, 0:1]
    grad_out[...] = direct - xg[voc, 0:rows, :].astype(F32) * back_col
    sums = gain_z[0]
    for j in range(1, NZ):
        arrive(gain_z.at[j], gain_sem, 2 + j)
        sums = sums + gain_z[j]
    gain_out[...] = sums[0:heads, :]
    spot = lax.broadcasted_iota(jnp.int32, loss_out.shape, 1)
    losses = jnp.zeros(loss_out.shape, F32)
    tokens = rows * NZ * PER_Z
    for h in range(heads):
        loss = jnp.sum(sums[heads : heads + 1, h * rows : (h + 1) * rows], axis=-1, keepdims=True)
        losses = losses + jnp.where(spot == h, loss / tokens, 0.0)
    loss_out[...] = losses
    for copy in pending:
        copy.wait_send()
    for i in range(2 * heads):
        for slot in range(12):
            x_copy(i, 0, slot).wait_send()
        for j in range(1, NY):
            y_copy(i, lax.rem(y + j, NY)).wait_send()


def per_device(hidden, head_weight, gains, unembed, targets, loss_weights):
    rows, cols = hidden.shape
    heads = gains.shape[0]
    voc_dev = unembed.shape[1]
    both = heads * rows
    runs = 2 * heads
    vmem = pl.BlockSpec(memory_space=pltpu.VMEM)
    dma = pltpu.SemaphoreType.DMA
    grad, gain, loss = pl.pallas_call(
        kernel,
        out_shape=(
            pltpu.VMEM((rows, cols), F32),
            pltpu.VMEM((heads, cols), F32),
            pltpu.VMEM((8, 128), F32),
        ),
        in_specs=[pl.BlockSpec(memory_space=pltpu.HBM)] * 6,
        out_specs=(vmem, vmem, vmem),
        scratch_shapes=[
            pltpu.VMEM(head_weight.shape, BF16),
            pltpu.VMEM(gains.shape, BF16),
            pltpu.VMEM(targets.shape, jnp.int32),
            pltpu.SMEM(loss_weights.shape, F32),
            pltpu.VMEM((NV, rows + 8 * heads, cols), BF16),
            pltpu.VMEM((NV, both, cols), BF16),
            pltpu.VMEM((heads, rows, NV * cols), BF16),
            pltpu.VMEM((NV * cols, voc_dev), BF16),
            pltpu.VMEM((2, rows // 2, voc_dev), BF16),
            pltpu.VMEM((both, voc_dev), F32),
            pltpu.VMEM((voc_dev, both), F32),
            pltpu.VMEM((voc_dev, both), BF16),
            pltpu.VMEM((heads, cols, rows), BF16),
            pltpu.VMEM((cols, rows), F32),
            pltpu.VMEM((heads, cols, rows), F32),
            pltpu.VMEM((rows, rows), F32),
            pltpu.VMEM((8, rows), F32),
            pltpu.VMEM((8, both), F32),
            pltpu.VMEM((8 * heads, cols), F32),
            pltpu.VMEM((NX, 8, both), F32),
            pltpu.VMEM((NY, 8, both), F32),
            pltpu.VMEM((NX, 8, rows), F32),
            pltpu.VMEM((NY, 8, rows), F32),
            pltpu.VMEM((4, 8, cols), F32),
            pltpu.VMEM((NZ, 8, cols), F32),
            pltpu.VMEM((runs, 12, cols, rows), BF16),
            pltpu.VMEM((runs, 12, cols, rows), BF16),
            pltpu.VMEM((heads, 4, cols, rows), F32),
            pltpu.VMEM((runs, 4, cols, rows), F32),
            pltpu.VMEM((runs, 4, cols, rows), BF16),
            pltpu.VMEM((runs, 4, cols, rows), BF16),
            pltpu.VMEM((heads, cols, rows), F32),
            pltpu.VMEM((heads, cols, rows), F32),
            dma((6,)),
            dma((2, 30)),
            dma((2, 30)),
            dma((2, 4)),
            dma((2, 28)),
            dma((2, 16)),
            dma((2, 6)),
            dma((2, 6)),
            dma((2, 10)),
            dma((runs, 2, 16)),
        ],
        compiler_params=pltpu.CompilerParams(
            collective_id=0, has_side_effects=True, vmem_limit_bytes=60 * 1024 * 1024
        ),
    )(hidden, head_weight, gains, unembed, targets, loss_weights)
    return loss[0, :heads], grad, gain


def solution(mesh):
    in_specs = (
        P("seq", "vocab"),
        P(None, None, "vocab"),
        P(None, "vocab"),
        P("seq", "vocab"),
        P(None, "seq"),
        P(),
    )
    out_specs = (P(), P("seq", "vocab"), P(None, "vocab"))
    return jax.shard_map(
        per_device, mesh=mesh, in_specs=in_specs, out_specs=out_specs, check_vma=False
    )
```

```python
import jax
import jax.numpy as jnp
from jax import lax
from jax.experimental import pallas as pl
from jax.experimental.pallas import tpu as pltpu
from jax.sharding import PartitionSpec as P

eps = 1e-05
NX, NY, NZ, NFAR, NCORE = 4, 4, 8, 2, 2
NV = NX * NY
PER_Z = NFAR * NCORE
MESH = pl.DeviceIdType.MESH
F32, BF16 = jnp.float32, jnp.bfloat16


def kernel(
    hidden_hbm, w_hbm, gains_hbm, unembed_hbm, targets_hbm, weights_hbm,
    grad_out, gain_out, loss_out,
    w, gains, targets, weights, xg, hf, normed, table, relay, acc, acc_t, up, low,
    x_t, gain_cols, rcol, r_line, lossrow, gain_rows,
    stat_x, stat_y, dot_x, dot_y, gain_p, gain_z,
    rs_send, rs_in, rs_part, rs_own, ys_send, ys_recv, head_grad, norm_grad,
    local_sem, xg_sem, hf_sem, far_sem, ring_sem, share_sem, stat_sem, dot_sem, gain_sem, rs_sem,
):
    rows, cols = hidden_hbm.shape
    heads = gains.shape[0]
    both = heads * rows
    voc_dev = unembed_hbm.shape[1]
    width = cols * NV
    seq, voc = lax.axis_index("seq"), lax.axis_index("vocab")
    x, y = lax.rem(voc, NX), lax.div(voc, NX)
    z, far, core = lax.div(seq, PER_Z), lax.rem(lax.div(seq, NCORE), NFAR), lax.rem(seq, NCORE)
    right, left, over = lax.rem(x + 1, NX), lax.rem(x + 3, NX), lax.rem(x + 2, NX)
    levels = NFAR * NY
    level = far * NY + y

    def at_x(j):
        return (seq, y * NX + lax.rem(x + j, NX))

    def at_y(j):
        return (seq, lax.rem(y + j, NY) * NX + x)

    def at_z(j):
        return (lax.rem(z + j, NZ) * PER_Z + far * NCORE + core, voc)

    def at_pair(k):
        other_far = 1 - far if k // 2 else far
        other_core = 1 - core if k % 2 else core
        return (z * PER_Z + other_far * NCORE + other_core, voc)

    def at_level(j):
        other = lax.rem(level + j + levels, levels)
        return (z * PER_Z + lax.div(other, NY) * NCORE + core, lax.rem(other, NY) * NX + x)

    pending = []

    def send(src, dst, sems, k, to):
        copy = pltpu.make_async_remote_copy(
            src_ref=src, dst_ref=dst, send_sem=sems.at[0, k], recv_sem=sems.at[1, k],
            device_id=to, device_id_type=MESH,
        )
        copy.start()
        pending.append(copy)

    def arrive(dst, sems, k):
        pltpu.make_async_remote_copy(
            src_ref=dst, dst_ref=dst, send_sem=sems.at[0, k], recv_sem=sems.at[1, k],
            device_id=at_x(1), device_id_type=MESH,
        ).wait_recv()

    own_rows = pl.ds(pl.multiple_of(seq * rows, rows), rows)
    fetches = [
        pltpu.make_async_copy(hidden_hbm, xg.at[voc, pl.ds(0, rows), :], local_sem.at[0]),
        pltpu.make_async_copy(unembed_hbm, table.at[own_rows, :], local_sem.at[1]),
        pltpu.make_async_copy(gains_hbm, gains, local_sem.at[2]),
        pltpu.make_async_copy(targets_hbm, targets, local_sem.at[3]),
        pltpu.make_async_copy(weights_hbm, weights, local_sem.at[4]),
        pltpu.make_async_copy(w_hbm, w, local_sem.at[5]),
    ]
    for fetch in fetches:
        fetch.start()
    barrier = pltpu.get_barrier_semaphore()
    partners = (
        [at_x(j) for j in range(1, NX)] + [at_y(j) for j in range(1, NY)]
        + [at_z(j) for j in range(1, NZ)] + [at_pair(k) for k in range(1, 4)]
        + [at_level(2), at_level(-2)]
    )
    for partner in partners:
        pl.semaphore_signal(barrier, inc=1, device_id=partner, device_id_type=MESH)
    for k in range(5):
        fetches[k].wait()
    gain_lines = gains[...].astype(F32)
    gain_pad = jnp.concatenate(
        [jnp.broadcast_to(gain_lines[h : h + 1], (8, cols)) for h in range(heads)], axis=0
    )
    xg[voc, rows : rows + 8 * heads, :] = gain_pad.astype(BF16)
    pl.semaphore_wait(barrier, len(partners))

    def row(q):
        return lax.rem(y + NY - q, NY) * NX

    def gather_begin(at, sems, base):
        for j in range(1, NY):
            send(at(voc), at(voc), sems, base + j - 1, at_y(j))
        send(at(voc), at(voc), sems, base + 3, at_x(1))
        send(at(voc), at(voc), sems, base + 7, at_x(NX - 1))

    def gather_row(at, sems, base, q):
        slot = row(q) + x
        arrive(at(slot), sems, base + q - 1)
        send(at(slot), at(slot), sems, base + 3 + q, at_x(1))
        send(at(slot), at(slot), sems, base + 7 + q, at_x(NX - 1))

    def gather_cross(at, sems, base, q):
        if q < 2:
            slot, k, to = row(q) + left, 3 + q, at_x(1)
        else:
            slot, k, to = row(q) + right, 7 + q, at_x(NX - 1)
        arrive(at(slot), sems, base + k)
        send(at(slot), at(slot), sems, base + 11 + q, to)

    def gather_end(at, sems, base):
        for q in (2, 3):
            arrive(at(row(q) + left), sems, base + 3 + q)
        for q in (0, 1):
            arrive(at(row(q) + right), sems, base + 7 + q)
        for q in range(NY):
            arrive(at(row(q) + over), sems, base + 11 + q)

    half = rows // 2
    pads = 8 * heads

    def x_at(t):
        return lambda slot: xg.at[slot, pl.ds(t * half, half + t * pads), :]

    def hf_at(t):
        return lambda slot: hf.at[slot, pl.ds(t * rows, rows), :]

    def slab(zz, e, own=True, first=0, count=rows):
        far_e = 1 - far if e else far
        core_e = core if own else 1 - core
        start = pl.multiple_of((zz * PER_Z + far_e * NCORE + core_e) * rows + first, count)
        return table.at[pl.ds(start, count), :]

    def z_at(j):
        return lax.rem(z + j + NZ, NZ)

    def share(e, k, zz):
        send(slab(zz, e), slab(zz, e), share_sem, e * NZ + k, at_pair(1))

    def part_of(zz, e, p):
        return slab(zz, e, True, p * half, half)

    leg = 2 - 4 * core

    def far_begin(p):
        send(part_of(z, 0, p), relay.at[p], far_sem, p, at_level(leg))

    def far_pass(p):
        arrive(relay.at[p], far_sem, p)
        source = lax.rem(level - leg + levels, levels)
        begin = (z * PER_Z + lax.div(source, NY) * NCORE + core) * rows + p * half
        place = table.at[pl.ds(pl.multiple_of(begin, half), half), :]
        send(relay.at[p], place, far_sem, 2 + p, at_level(leg))

    def ring_send(zz, e, way, h, p):
        block = part_of(zz, e, p)
        send(block, block, ring_sem, e * 14 + way * 7 + (h - 1) * 2 + (p if h < 4 else 0),
             at_z(NZ - 1 if way else 1))

    def ring_arrive(zz, e, way, h, p):
        arrive(part_of(zz, e, p), ring_sem, e * 14 + way * 7 + (h - 1) * 2 + (p if h < 4 else 0))

    def ring_begin(e, turn):
        if e:
            arrive(part_of(z, 1, turn), far_sem, 2 + turn)
        for way in range(2):
            ring_send(z, e, way, 1, turn if e else way ^ turn)
        if turn:
            share(e, 0, z)

    def ring_step(e, h, turn):
        for way in range(2):
            p = turn if e and h == 1 else way ^ turn
            zz = z_at(h if way else -h)
            ring_arrive(zz, e, way, h, p)
            if h < 3 or p == way:
                ring_send(zz, e, way, h + 1, p)
            if turn:
                share(e, 2 * h - 1 + way, zz)

    def ring_end(e):
        zz = z_at(4)
        for way in range(2):
            ring_arrive(zz, e, way, 4, way)
        share(e, 7, zz)

    def consume(e, first, last):
        far_e = 1 - far if e else far

        def body(k, carry):
            dist = lax.div(k + 1, 2)
            zz = lax.rem(z + NZ + dist * (1 - 2 * lax.rem(k, 2)), NZ)
            arrive(slab(zz, e, False), share_sem, e * NZ + k)
            block = zz * NFAR + far_e
            begin = pl.multiple_of(block * cols, cols)
            lines = [
                hf[block, t * rows + h * half : t * rows + (h + 1) * half, :]
                for h in range(heads) for t in range(2)
            ]
            acc[...] += jnp.dot(
                jnp.concatenate(lines, axis=0), table[pl.ds(begin, cols), :],
                preferred_element_type=F32,
            )
            return carry

        lax.fori_loop(first, last, body, 0)

    for k, t in enumerate((1, 0)):
        gather_begin(x_at(t), xg_sem, 15 * t)
        ring_begin(0, k)
        far_begin(k)

    acc[...] = jnp.zeros_like(acc)
    own_x = xg[voc, 0:rows, :].astype(F32)
    x_t[...] = own_x.T
    for h in range(heads):
        gain_cols[h] = jnp.broadcast_to(gain_lines[h : h + 1], (rows, cols)).T

    def project(t, between):
        lo = t * half

        def square(k, total):
            block = xg[k, lo : lo + half, :].astype(F32)
            return total + block * block

        squares = lax.fori_loop(0, NV, square, jnp.zeros((half, cols), F32))
        r = lax.rsqrt(jnp.sum(squares, axis=-1, keepdims=True) / width + eps)
        rcol[lo : lo + half, :] = jnp.broadcast_to(r, (half, rows))

        def norm(k, carry):
            scaled = xg[k, lo : lo + half, :].astype(F32) * rcol[lo : lo + half, 0:1]
            begin = pl.multiple_of(k * cols, cols)
            gain_k = xg[k, rows : rows + pads, :].astype(F32)
            for h in range(heads):
                line = (scaled * gain_k[8 * h : 8 * h + 1]).astype(BF16)
                normed[h, lo : lo + half, pl.ds(begin, cols)] = line
            return carry

        between(0)
        lax.fori_loop(0, NV, norm, 0)
        for h in range(heads):
            between(1 + h)
            branch = jnp.dot(normed[h, lo : lo + half, :], w[h], preferred_element_type=F32)
            total = xg[voc, lo : lo + half, :].astype(F32) + branch
            at = t * rows + h * half
            hf[voc, at : at + half, :] = total.astype(BF16)
        gather_begin(hf_at(t), hf_sem, 15 * t)

    def rows_of(at, sems, base):
        for q in range(1, NY):
            gather_row(at, sems, base, q)

    def cross_of(at, sems, base):
        for q in (0, 2, 1, 3):
            gather_cross(at, sems, base, q)

    def first_between(k):
        if k == 1:
            ring_step(0, 3, 0)

    def second_between(k):
        if k == 0:
            ring_step(0, 3, 1)
        if k == 1:
            ring_step(1, 1, 0)
        if k == 2:
            rows_of(hf_at(1), hf_sem, 15)

    rows_of(x_at(1), xg_sem, 15)
    ring_step(0, 1, 0)
    far_pass(0)
    rows_of(x_at(0), xg_sem, 0)
    cross_of(x_at(1), xg_sem, 15)
    ring_step(0, 1, 1)
    far_pass(1)
    ring_step(0, 2, 0)
    cross_of(x_at(0), xg_sem, 0)
    ring_begin(1, 0)
    gather_end(x_at(1), xg_sem, 15)
    ring_step(0, 2, 1)
    ring_begin(1, 1)
    fetches[5].wait()
    project(1, first_between)
    gather_end(x_at(0), xg_sem, 0)
    project(0, second_between)
    ring_step(1, 1, 1)
    r_line[...] = rcol[...].T[0:8, :]
    ring_end(0)
    cross_of(hf_at(1), hf_sem, 15)
    ring_step(1, 2, 0)
    rows_of(hf_at(0), hf_sem, 0)
    ring_step(1, 2, 1)
    cross_of(hf_at(0), hf_sem, 0)
    gather_end(hf_at(1), hf_sem, 15)
    ring_step(1, 3, 0)
    gather_end(hf_at(0), hf_sem, 0)

    consume(0, 0, 4)
    ring_step(1, 3, 1)
    consume(0, 4, NZ)
    consume(1, 0, 7)
    ring_end(1)
    consume(1, 7, NZ)

    step = 128
    ids = jnp.concatenate([targets[h : h + 1, :] for h in range(heads)], axis=1) - voc * voc_dev
    chunk_ids = lax.broadcasted_iota(jnp.int32, (step, both), 0)
    lane = lax.broadcasted_iota(jnp.int32, (1, both), 1)
    weight_row = jnp.full((1, both), weights[0], F32)
    for h in range(1, heads):
        weight_row = jnp.where(lane >= h * rows, weights[h], weight_row)

    def stat_rows(top, total, target):
        line = lax.broadcasted_iota(jnp.int32, (8, both), 0)
        return jnp.where(line == 0, top, jnp.where(line == 1, total, jnp.where(line == 2, target, 0.0)))

    def merge(slots, count):
        tops = [slots[j, 0:1, :] for j in range(count)]
        top = tops[0]
        for other in tops[1:]:
            top = jnp.maximum(top, other)
        total = jnp.zeros_like(top)
        target = jnp.zeros_like(top)
        for j in range(count):
            total = total + slots[j, 1:2, :] * jnp.exp(tops[j] - top)
            target = target + slots[j, 2:3, :]
        return top, total, target

    def turn(k, top):
        begin = pl.multiple_of(k * step, step)
        chunk = acc[:, pl.ds(begin, step)].T
        acc_t[pl.ds(begin, step), :] = chunk
        return jnp.maximum(top, jnp.max(chunk, axis=0, keepdims=True))

    first_chunk = acc[:, 0:step].T
    acc_t[0:step, :] = first_chunk
    top = lax.fori_loop(1, voc_dev // step, turn, jnp.max(first_chunk, axis=0, keepdims=True))

    def gauge(k, sums):
        begin = pl.multiple_of(k * step, step)
        chunk = acc_t[pl.ds(begin, step), :]
        total = jnp.sum(jnp.exp(chunk - top), axis=0, keepdims=True)
        hit = jnp.where(chunk_ids == ids - begin, chunk, 0.0)
        return sums[0] + total, sums[1] + jnp.sum(hit, axis=0, keepdims=True)

    empty = jnp.zeros((1, both), F32)
    total, target = lax.fori_loop(0, voc_dev // step, gauge, (empty, empty))
    stat_x[0] = stat_rows(top, total, target)
    for j in range(1, NX):
        send(stat_x.at[0], stat_x.at[j], stat_sem, j - 1, at_x(j))
    for j in range(1, NX):
        arrive(stat_x.at[j], stat_sem, j - 1)
    stat_y[0] = stat_rows(*merge(stat_x, NX))
    for j in range(1, NY):
        send(stat_y.at[0], stat_y.at[j], stat_sem, 2 + j, at_y(j))
    for j in range(1, NY):
        arrive(stat_y.at[j], stat_sem, 2 + j)
    top, total, target = merge(stat_y, NY)
    lse = top + jnp.log(total)
    lossrow[...] = jnp.broadcast_to(lse - target, lossrow.shape)

    def pull(k, carry):
        begin = pl.multiple_of(k * step, step)
        probs = jnp.exp(acc_t[pl.ds(begin, step), :] - lse)
        hit = jnp.where(chunk_ids == ids - begin, 1.0, 0.0)
        up[pl.ds(begin, step), :] = (weight_row * (probs - hit)).astype(BF16)
        return carry

    lax.fori_loop(0, voc_dev // step, pull, 0)

    def block_rows(way, yb):
        block = yb * NX + lax.rem(x + way, NX)
        return pl.ds(pl.multiple_of(block * cols, cols), cols)

    def head_part(way, yb):
        out = jnp.dot(table[block_rows(way, yb), :], up[...], preferred_element_type=F32)
        return [out[:, h * rows : (h + 1) * rows] for h in range(heads)]

    def norm_part(h, way, yb):
        return jnp.dot(w[h, block_rows(way, yb), :], low[h], preferred_element_type=F32)

    def across_of(n):
        way, b = lax.rem(n, 2), lax.div(n, 2)
        return way, 2 * way + b, 2 * way + b

    def near_of(n):
        way, b = lax.rem(n, 2), lax.div(n, 2)
        yb = 2 - 2 * way + b
        return way, yb, 4 + 4 * way + yb

    def last_of(n):
        way, b = lax.rem(n, 2), lax.div(n, 2)
        yb = 2 * way + b
        return way, yb, 4 + 4 * way + yb

    def loop4(body):
        def run(n, carry):
            body(n)
            return carry

        lax.fori_loop(0, 4, run, 0)

    def x_copy(i, way, slot):
        return pltpu.make_async_remote_copy(
            src_ref=rs_send.at[i, slot], dst_ref=rs_in.at[i, slot],
            send_sem=rs_sem.at[i, 0, slot], recv_sem=rs_sem.at[i, 1, slot],
            device_id=at_x(1 + 2 * way), device_id_type=MESH,
        )

    def x_arrive(i, slot):
        x_copy(i, 0, slot).wait_recv()

    def y_copy(i, yb):
        return pltpu.make_async_remote_copy(
            src_ref=ys_send.at[i, yb], dst_ref=ys_recv.at[i, y],
            send_sem=rs_sem.at[i, 0, 12 + yb], recv_sem=rs_sem.at[i, 1, 12 + y],
            device_id=(seq, yb * NX + x), device_id_type=MESH,
        )

    def y_arrive(i, yb):
        pltpu.make_async_remote_copy(
            src_ref=ys_send.at[i, yb], dst_ref=ys_recv.at[i, yb],
            send_sem=rs_sem.at[i, 0, 12 + yb], recv_sem=rs_sem.at[i, 1, 12 + yb],
            device_id=(seq, yb * NX + x), device_id_type=MESH,
        ).wait_recv()

    def column(i):
        for k in range(2):
            for yb in (k, k + 2):
                x_arrive(i, 4 + yb)
                x_arrive(i, 8 + yb)
                total = rs_own[i, yb] + rs_in[i, 4 + yb].astype(F32) + rs_in[i, 8 + yb].astype(F32)
                rs_own[i, yb] = total
                ys_send[i, yb] = total.astype(BF16)

                @pl.when(y != yb)
                def _():
                    y_copy(i, yb).start()

    def finish(i):
        total = rs_own[i, y]
        for j in range(1, NY):
            peer = lax.rem(y + j, NY)
            y_arrive(i, peer)
            total = total + ys_recv[i, peer].astype(F32)
        return total

    def across_heads(n):
        way, yb, slot = across_of(n)
        for h, part in enumerate(head_part(2, yb)):
            rs_send[h, slot] = part.astype(BF16)
        x_copy(0, way, slot).start()

    def near_heads(n):
        way, yb, slot = near_of(n)
        for h, part in enumerate(head_part(1 + 2 * way, yb)):
            rs_send[h, slot] = part.astype(BF16)
        x_copy(0, way, slot).start()

    def last_heads(n):
        way, yb, slot = last_of(n)
        for h, part in enumerate(head_part(1 + 2 * way, yb)):
            rs_part[h, yb] = part

    def own_heads(n):
        for h, part in enumerate(head_part(0, n)):
            rs_own[h, n] = part

    def send_heads(h):
        def across(n):
            way, yb, slot = across_of(n)
            x_copy(h, way, slot).start()

        def near(n):
            way, yb, slot = near_of(n)
            x_copy(h, way, slot).start()

        loop4(across)
        loop4(near)

    def pass_heads(h):
        def body(n):
            way, yb, slot = last_of(n)
            x_arrive(h, yb)
            rs_send[h, slot] = (rs_part[h, yb] + rs_in[h, yb].astype(F32)).astype(BF16)
            x_copy(h, way, slot).start()

        loop4(body)

    def head_done(h):
        total = finish(h)
        low[h] = total.astype(BF16)
        head_grad[h] = total

    def norm_begin(h):
        i = heads + h

        def across(n):
            way, yb, slot = across_of(n)
            rs_send[i, slot] = norm_part(h, 2, yb).astype(BF16)
            x_copy(i, way, slot).start()

        def near(n):
            way, yb, slot = near_of(n)
            rs_send[i, slot] = norm_part(h, 1 + 2 * way, yb).astype(BF16)
            x_copy(i, way, slot).start()

        loop4(across)
        loop4(near)

    def norm_pass(h):
        i = heads + h

        def own(n):
            rs_own[i, n] = norm_part(h, 0, n)

        def last(n):
            way, yb, slot = last_of(n)
            part = norm_part(h, 1 + 2 * way, yb)
            x_arrive(i, yb)
            rs_send[i, slot] = (part + rs_in[i, yb].astype(F32)).astype(BF16)
            x_copy(i, way, slot).start()

        loop4(own)
        loop4(last)

    def norm_done(h):
        norm_grad[h] = finish(heads + h)

    def gain_done(h):
        weighed = norm_grad[h] * x_t[...] * r_line[0:1, :]
        part = jnp.sum(weighed.T, axis=0, keepdims=True)
        gain_rows[8 * h : 8 * h + 8, :] = jnp.broadcast_to(part, (8, cols))

    def left_x(i):
        for slot in range(12):
            x_copy(i, 0, slot).wait_send()

    def left_y(i):
        for j in range(1, NY):
            y_copy(i, lax.rem(y + j, NY)).wait_send()

    loop4(across_heads)
    loop4(near_heads)
    loop4(last_heads)
    pass_heads(0)
    send_heads(1)
    loop4(own_heads)
    column(0)
    pass_heads(1)
    head_done(0)
    norm_begin(0)
    column(1)
    norm_pass(0)
    for copy in pending:
        copy.wait_send()
    pending.clear()
    left_x(0)
    left_y(0)
    left_x(1)
    head_done(1)
    norm_begin(1)
    column(2)
    norm_pass(1)
    left_y(1)
    left_x(2)
    norm_done(0)
    gain_done(0)
    column(3)
    norm_done(1)

    for h in range(1, heads):
        gain_done(h)
    line = lax.broadcasted_iota(jnp.int32, (8, cols), 0)
    packed = jnp.where(line == heads, lossrow[...], 0.0)
    for h in range(heads):
        packed = packed + jnp.where(line == h, gain_rows[8 * h : 8 * h + 8, :], 0.0)
    gain_p[0] = packed
    for k in (2, 3, 1):
        send(gain_p.at[0], gain_p.at[k], gain_sem, k - 1, at_pair(k))
    scaled = jnp.zeros((cols, rows), F32)
    for h in range(heads):
        scaled = scaled + gain_cols[h] * norm_grad[h]
    dots = jnp.sum(scaled * x_t[...], axis=0, keepdims=True)
    dot_x[0] = jnp.broadcast_to(dots, (8, rows))
    for j in range(1, NX):
        send(dot_x.at[0], dot_x.at[j], dot_sem, j - 1, at_x(j))
    for j in range(1, NX):
        arrive(dot_x.at[j], dot_sem, j - 1)
    dot_y[0] = dot_x[0] + dot_x[1] + dot_x[2] + dot_x[3]
    for j in range(1, NY):
        send(dot_y.at[0], dot_y.at[j], dot_sem, 2 + j, at_y(j))
    r_row = r_line[0:1, :]
    direct = (head_grad[0] + head_grad[1] + r_row * scaled).T
    for k in range(1, 4):
        arrive(gain_p.at[k], gain_sem, k - 1)
    gain_z[0] = gain_p[0] + gain_p[1] + gain_p[2] + gain_p[3]
    for j in range(1, NZ):
        send(gain_z.at[0], gain_z.at[j], gain_sem, 2 + j, at_z(j))
    for j in range(1, NY):
        arrive(dot_y.at[j], dot_sem, 2 + j)
    dots = dot_y[0] + dot_y[1] + dot_y[2] + dot_y[3]
    back = r_row * r_row * r_row * dots[0:1, :] / width
    back_col = jnp.broadcast_to(back, (rows, rows)).T[:, 0:1]
    grad_out[...] = direct - xg[voc, 0:rows, :].astype(F32) * back_col
    sums = gain_z[0]
    for j in range(1, NZ):
        arrive(gain_z.at[j], gain_sem, 2 + j)
        sums = sums + gain_z[j]
    gain_out[...] = sums[0:heads, :]
    spot = lax.broadcasted_iota(jnp.int32, loss_out.shape, 1)
    losses = jnp.zeros(loss_out.shape, F32)
    tokens = rows * NZ * PER_Z
    for h in range(heads):
        loss = jnp.sum(sums[heads : heads + 1, h * rows : (h + 1) * rows], axis=-1, keepdims=True)
        losses = losses + jnp.where(spot == h, loss / tokens, 0.0)
    loss_out[...] = losses
    for copy in pending:
        copy.wait_send()
    left_y(2)
    left_x(3)
    left_y(3)


def per_device(hidden, head_weight, gains, unembed, targets, loss_weights):
    rows, cols = hidden.shape
    heads = gains.shape[0]
    voc_dev = unembed.shape[1]
    both = heads * rows
    runs = 2 * heads
    vmem = pl.BlockSpec(memory_space=pltpu.VMEM)
    dma = pltpu.SemaphoreType.DMA
    grad, gain, loss = pl.pallas_call(
        kernel,
        out_shape=(
            pltpu.VMEM((rows, cols), F32),
            pltpu.VMEM((heads, cols), F32),
            pltpu.VMEM((8, 128), F32),
        ),
        in_specs=[pl.BlockSpec(memory_space=pltpu.HBM)] * 6,
        out_specs=(vmem, vmem, vmem),
        scratch_shapes=[
            pltpu.VMEM(head_weight.shape, BF16),
            pltpu.VMEM(gains.shape, BF16),
            pltpu.VMEM(targets.shape, jnp.int32),
            pltpu.SMEM(loss_weights.shape, F32),
            pltpu.VMEM((NV, rows + 8 * heads, cols), BF16),
            pltpu.VMEM((NV, both, cols), BF16),
            pltpu.VMEM((heads, rows, NV * cols), BF16),
            pltpu.VMEM((NV * cols, voc_dev), BF16),
            pltpu.VMEM((2, rows // 2, voc_dev), BF16),
            pltpu.VMEM((both, voc_dev), F32),
            pltpu.VMEM((voc_dev, both), F32),
            pltpu.VMEM((voc_dev, both), BF16),
            pltpu.VMEM((heads, cols, rows), BF16),
            pltpu.VMEM((cols, rows), F32),
            pltpu.VMEM((heads, cols, rows), F32),
            pltpu.VMEM((rows, rows), F32),
            pltpu.VMEM((8, rows), F32),
            pltpu.VMEM((8, both), F32),
            pltpu.VMEM((8 * heads, cols), F32),
            pltpu.VMEM((NX, 8, both), F32),
            pltpu.VMEM((NY, 8, both), F32),
            pltpu.VMEM((NX, 8, rows), F32),
            pltpu.VMEM((NY, 8, rows), F32),
            pltpu.VMEM((4, 8, cols), F32),
            pltpu.VMEM((NZ, 8, cols), F32),
            pltpu.VMEM((runs, 12, cols, rows), BF16),
            pltpu.VMEM((runs, 12, cols, rows), BF16),
            pltpu.VMEM((heads, 4, cols, rows), F32),
            pltpu.VMEM((runs, 4, cols, rows), F32),
            pltpu.VMEM((runs, 4, cols, rows), BF16),
            pltpu.VMEM((runs, 4, cols, rows), BF16),
            pltpu.VMEM((heads, cols, rows), F32),
            pltpu.VMEM((heads, cols, rows), F32),
            dma((6,)),
            dma((2, 30)),
            dma((2, 30)),
            dma((2, 4)),
            dma((2, 28)),
            dma((2, 16)),
            dma((2, 6)),
            dma((2, 6)),
            dma((2, 10)),
            dma((runs, 2, 16)),
        ],
        compiler_params=pltpu.CompilerParams(
            collective_id=0, has_side_effects=True, vmem_limit_bytes=60 * 1024 * 1024
        ),
    )(hidden, head_weight, gains, unembed, targets, loss_weights)
    return loss[0, :heads], grad, gain


def solution(mesh):
    in_specs = (
        P("seq", "vocab"),
        P(None, None, "vocab"),
        P(None, "vocab"),
        P("seq", "vocab"),
        P(None, "seq"),
        P(),
    )
    out_specs = (P(), P("seq", "vocab"), P(None, "vocab"))
    return jax.shard_map(
        per_device, mesh=mesh, in_specs=in_specs, out_specs=out_specs, check_vma=False
    )
```

```python
import jax
import jax.numpy as jnp
from jax import lax
from jax.experimental import pallas as pl
from jax.experimental.pallas import tpu as pltpu
from jax.sharding import PartitionSpec as P

eps = 1e-05
NX, NY, NZ, NFAR, NCORE = 4, 4, 8, 2, 2
NV = NX * NY
PER_Z = NFAR * NCORE
MESH = pl.DeviceIdType.MESH
F32, BF16 = jnp.float32, jnp.bfloat16


def kernel(
    hidden_hbm, w_hbm, gains_hbm, unembed_hbm, targets_hbm, weights_hbm,
    grad_out, gain_out, loss_out,
    w, gains, targets, weights, xg, hf, normed, table, relay, acc, acc_t, up, low,
    x_t, gain_cols, rcol, r_line, lossrow, gain_rows,
    stat_x, stat_y, dot_x, dot_y, gain_p, gain_z,
    rs_send, rs_in, rs_part, rs_own, ys_send, ys_recv, head_grad, norm_grad,
    local_sem, xg_sem, hf_sem, far_sem, ring_sem, share_sem, stat_sem, dot_sem, gain_sem, rs_sem,
):
    rows, cols = hidden_hbm.shape
    heads = gains.shape[0]
    both = heads * rows
    voc_dev = unembed_hbm.shape[1]
    width = cols * NV
    seq, voc = lax.axis_index("seq"), lax.axis_index("vocab")
    x, y = lax.rem(voc, NX), lax.div(voc, NX)
    z, far, core = lax.div(seq, PER_Z), lax.rem(lax.div(seq, NCORE), NFAR), lax.rem(seq, NCORE)
    right, left, over = lax.rem(x + 1, NX), lax.rem(x + 3, NX), lax.rem(x + 2, NX)
    levels = NFAR * NY
    level = far * NY + y

    def at_x(j):
        return (seq, y * NX + lax.rem(x + j, NX))

    def at_y(j):
        return (seq, lax.rem(y + j, NY) * NX + x)

    def at_z(j):
        return (lax.rem(z + j, NZ) * PER_Z + far * NCORE + core, voc)

    def at_pair(k):
        other_far = 1 - far if k // 2 else far
        other_core = 1 - core if k % 2 else core
        return (z * PER_Z + other_far * NCORE + other_core, voc)

    def at_level(j):
        other = lax.rem(level + j + levels, levels)
        return (z * PER_Z + lax.div(other, NY) * NCORE + core, lax.rem(other, NY) * NX + x)

    pending = []

    def send(src, dst, sems, k, to):
        copy = pltpu.make_async_remote_copy(
            src_ref=src, dst_ref=dst, send_sem=sems.at[0, k], recv_sem=sems.at[1, k],
            device_id=to, device_id_type=MESH,
        )
        copy.start()
        pending.append(copy)

    def arrive(dst, sems, k):
        pltpu.make_async_remote_copy(
            src_ref=dst, dst_ref=dst, send_sem=sems.at[0, k], recv_sem=sems.at[1, k],
            device_id=at_x(1), device_id_type=MESH,
        ).wait_recv()

    own_rows = pl.ds(pl.multiple_of(seq * rows, rows), rows)
    fetches = [
        pltpu.make_async_copy(hidden_hbm, xg.at[voc, pl.ds(0, rows), :], local_sem.at[0]),
        pltpu.make_async_copy(unembed_hbm, table.at[own_rows, :], local_sem.at[1]),
        pltpu.make_async_copy(gains_hbm, gains, local_sem.at[2]),
        pltpu.make_async_copy(targets_hbm, targets, local_sem.at[3]),
        pltpu.make_async_copy(weights_hbm, weights, local_sem.at[4]),
        pltpu.make_async_copy(w_hbm, w, local_sem.at[5]),
    ]
    for fetch in fetches:
        fetch.start()
    barrier = pltpu.get_barrier_semaphore()
    partners = (
        [at_x(j) for j in range(1, NX)] + [at_y(j) for j in range(1, NY)]
        + [at_z(j) for j in range(1, NZ)] + [at_pair(k) for k in range(1, 4)]
        + [at_level(2), at_level(-2)]
    )
    for partner in partners:
        pl.semaphore_signal(barrier, inc=1, device_id=partner, device_id_type=MESH)
    for k in range(5):
        fetches[k].wait()
    gain_lines = gains[...].astype(F32)
    gain_pad = jnp.concatenate(
        [jnp.broadcast_to(gain_lines[h : h + 1], (8, cols)) for h in range(heads)], axis=0
    )
    xg[voc, rows : rows + 8 * heads, :] = gain_pad.astype(BF16)
    pl.semaphore_wait(barrier, len(partners))

    def row(q):
        return lax.rem(y + NY - q, NY) * NX

    def gather_begin(at, sems, base):
        for j in range(1, NY):
            send(at(voc), at(voc), sems, base + j - 1, at_y(j))
        send(at(voc), at(voc), sems, base + 3, at_x(1))
        send(at(voc), at(voc), sems, base + 7, at_x(NX - 1))

    def gather_row(at, sems, base, q):
        slot = row(q) + x
        arrive(at(slot), sems, base + q - 1)
        send(at(slot), at(slot), sems, base + 3 + q, at_x(1))
        send(at(slot), at(slot), sems, base + 7 + q, at_x(NX - 1))

    def gather_cross(at, sems, base, q):
        if q < 2:
            slot, k, to = row(q) + left, 3 + q, at_x(1)
        else:
            slot, k, to = row(q) + right, 7 + q, at_x(NX - 1)
        arrive(at(slot), sems, base + k)
        send(at(slot), at(slot), sems, base + 11 + q, to)

    def gather_end(at, sems, base):
        for q in (2, 3):
            arrive(at(row(q) + left), sems, base + 3 + q)
        for q in (0, 1):
            arrive(at(row(q) + right), sems, base + 7 + q)
        for q in range(NY):
            arrive(at(row(q) + over), sems, base + 11 + q)

    half = rows // 2
    pads = 8 * heads

    def x_at(t):
        return lambda slot: xg.at[slot, pl.ds(t * half, half + t * pads), :]

    def hf_at(t):
        return lambda slot: hf.at[slot, pl.ds(t * rows, rows), :]

    def slab(zz, e, own=True, first=0, count=rows):
        far_e = 1 - far if e else far
        core_e = core if own else 1 - core
        start = pl.multiple_of((zz * PER_Z + far_e * NCORE + core_e) * rows + first, count)
        return table.at[pl.ds(start, count), :]

    def z_at(j):
        return lax.rem(z + j + NZ, NZ)

    def share(e, k, zz):
        send(slab(zz, e), slab(zz, e), share_sem, e * NZ + k, at_pair(1))

    def part_of(zz, e, p):
        return slab(zz, e, True, p * half, half)

    leg = 2 - 4 * core

    def far_begin(p):
        send(part_of(z, 0, p), relay.at[p], far_sem, p, at_level(leg))

    def far_pass(p):
        arrive(relay.at[p], far_sem, p)
        source = lax.rem(level - leg + levels, levels)
        begin = (z * PER_Z + lax.div(source, NY) * NCORE + core) * rows + p * half
        place = table.at[pl.ds(pl.multiple_of(begin, half), half), :]
        send(relay.at[p], place, far_sem, 2 + p, at_level(leg))

    def ring_send(zz, e, way, h, p):
        block = part_of(zz, e, p)
        send(block, block, ring_sem, e * 14 + way * 7 + (h - 1) * 2 + (p if h < 4 else 0),
             at_z(NZ - 1 if way else 1))

    def ring_arrive(zz, e, way, h, p):
        arrive(part_of(zz, e, p), ring_sem, e * 14 + way * 7 + (h - 1) * 2 + (p if h < 4 else 0))

    def ring_begin(e, turn):
        if e:
            arrive(part_of(z, 1, turn), far_sem, 2 + turn)
        for way in range(2):
            ring_send(z, e, way, 1, turn if e else way ^ turn)
        if turn:
            share(e, 0, z)

    def ring_step(e, h, turn):
        for way in range(2):
            p = turn if e and h == 1 else way ^ turn
            zz = z_at(h if way else -h)
            ring_arrive(zz, e, way, h, p)
            if h < 3 or p == way:
                ring_send(zz, e, way, h + 1, p)
            if turn:
                share(e, 2 * h - 1 + way, zz)

    def ring_end(e):
        zz = z_at(4)
        for way in range(2):
            ring_arrive(zz, e, way, 4, way)
        share(e, 7, zz)

    def consume(e, slabs):
        far_e = 1 - far if e else far
        left_parts, right_parts = [], []
        for k in slabs:
            zz = z_at((k + 1) // 2 * (1 - 2 * (k % 2)))
            arrive(slab(zz, e, False), share_sem, e * NZ + k)
            block = zz * NFAR + far_e
            lines = [
                hf[block, t * rows + h * half : t * rows + (h + 1) * half, :]
                for h in range(heads) for t in range(2)
            ]
            left_parts.append(jnp.concatenate(lines, axis=0))
            right_parts.append(table[pl.ds(pl.multiple_of(block * cols, cols), cols), :])
        acc[...] += jnp.dot(
            jnp.concatenate(left_parts, axis=1), jnp.concatenate(right_parts, axis=0),
            preferred_element_type=F32,
        )

    for k, t in enumerate((1, 0)):
        gather_begin(x_at(t), xg_sem, 15 * t)
        ring_begin(0, k)
        far_begin(k)

    acc[...] = jnp.zeros_like(acc)
    own_x = xg[voc, 0:rows, :].astype(F32)
    x_t[...] = own_x.T
    for h in range(heads):
        gain_cols[h] = jnp.broadcast_to(gain_lines[h : h + 1], (rows, cols)).T

    def project(t, between):
        lo = t * half

        def square(k, total):
            block = xg[k, lo : lo + half, :].astype(F32)
            return total + block * block

        squares = lax.fori_loop(0, NV, square, jnp.zeros((half, cols), F32))
        r = lax.rsqrt(jnp.sum(squares, axis=-1, keepdims=True) / width + eps)
        rcol[lo : lo + half, :] = jnp.broadcast_to(r, (half, rows))

        def norm(k, carry):
            scaled = xg[k, lo : lo + half, :].astype(F32) * rcol[lo : lo + half, 0:1]
            begin = pl.multiple_of(k * cols, cols)
            gain_k = xg[k, rows : rows + pads, :].astype(F32)
            for h in range(heads):
                line = (scaled * gain_k[8 * h : 8 * h + 1]).astype(BF16)
                normed[h, lo : lo + half, pl.ds(begin, cols)] = line
            return carry

        between(0)
        lax.fori_loop(0, NV, norm, 0)
        for h in range(heads):
            between(1 + h)
            branch = jnp.dot(normed[h, lo : lo + half, :], w[h], preferred_element_type=F32)
            total = xg[voc, lo : lo + half, :].astype(F32) + branch
            at = t * rows + h * half
            hf[voc, at : at + half, :] = total.astype(BF16)
        gather_begin(hf_at(t), hf_sem, 15 * t)

    def rows_of(at, sems, base):
        for q in range(1, NY):
            gather_row(at, sems, base, q)

    def cross_of(at, sems, base):
        for q in (0, 2, 1, 3):
            gather_cross(at, sems, base, q)

    def first_between(k):
        if k == 1:
            ring_step(0, 3, 0)

    def second_between(k):
        if k == 0:
            ring_step(0, 3, 1)
        if k == 1:
            ring_step(1, 1, 0)
        if k == 2:
            rows_of(hf_at(1), hf_sem, 15)

    rows_of(x_at(1), xg_sem, 15)
    ring_step(0, 1, 0)
    far_pass(0)
    rows_of(x_at(0), xg_sem, 0)
    cross_of(x_at(1), xg_sem, 15)
    ring_step(0, 1, 1)
    far_pass(1)
    ring_step(0, 2, 0)
    cross_of(x_at(0), xg_sem, 0)
    ring_begin(1, 0)
    gather_end(x_at(1), xg_sem, 15)
    ring_step(0, 2, 1)
    ring_begin(1, 1)
    fetches[5].wait()
    project(1, first_between)
    gather_end(x_at(0), xg_sem, 0)
    project(0, second_between)
    ring_step(1, 1, 1)
    r_line[...] = rcol[...].T[0:8, :]
    ring_end(0)
    cross_of(hf_at(1), hf_sem, 15)
    ring_step(1, 2, 0)
    rows_of(hf_at(0), hf_sem, 0)
    ring_step(1, 2, 1)
    cross_of(hf_at(0), hf_sem, 0)
    gather_end(hf_at(1), hf_sem, 15)
    ring_step(1, 3, 0)
    gather_end(hf_at(0), hf_sem, 0)

    consume(0, (0, 1, 2, 3))
    ring_step(1, 3, 1)
    consume(0, (4, 5, 6, 7))
    consume(1, (0, 1, 2))
    consume(1, (3, 4, 5, 6))
    ring_end(1)
    consume(1, (7,))

    step = 128
    ids = jnp.concatenate([targets[h : h + 1, :] for h in range(heads)], axis=1) - voc * voc_dev
    chunk_ids = lax.broadcasted_iota(jnp.int32, (step, both), 0)
    lane = lax.broadcasted_iota(jnp.int32, (1, both), 1)
    weight_row = jnp.full((1, both), weights[0], F32)
    for h in range(1, heads):
        weight_row = jnp.where(lane >= h * rows, weights[h], weight_row)

    def stat_rows(top, total, target):
        line = lax.broadcasted_iota(jnp.int32, (8, both), 0)
        return jnp.where(line == 0, top, jnp.where(line == 1, total, jnp.where(line == 2, target, 0.0)))

    def merge(slots, count):
        tops = [slots[j, 0:1, :] for j in range(count)]
        top = tops[0]
        for other in tops[1:]:
            top = jnp.maximum(top, other)
        total = jnp.zeros_like(top)
        target = jnp.zeros_like(top)
        for j in range(count):
            total = total + slots[j, 1:2, :] * jnp.exp(tops[j] - top)
            target = target + slots[j, 2:3, :]
        return top, total, target

    def turn(k, top):
        begin = pl.multiple_of(k * step, step)
        chunk = acc[:, pl.ds(begin, step)].T
        acc_t[pl.ds(begin, step), :] = chunk
        return jnp.maximum(top, jnp.max(chunk, axis=0, keepdims=True))

    first_chunk = acc[:, 0:step].T
    acc_t[0:step, :] = first_chunk
    top = lax.fori_loop(1, voc_dev // step, turn, jnp.max(first_chunk, axis=0, keepdims=True))

    def gauge(k, sums):
        begin = pl.multiple_of(k * step, step)
        chunk = acc_t[pl.ds(begin, step), :]
        total = jnp.sum(jnp.exp(chunk - top), axis=0, keepdims=True)
        hit = jnp.where(chunk_ids == ids - begin, chunk, 0.0)
        return sums[0] + total, sums[1] + jnp.sum(hit, axis=0, keepdims=True)

    empty = jnp.zeros((1, both), F32)
    total, target = lax.fori_loop(0, voc_dev // step, gauge, (empty, empty))
    stat_x[0] = stat_rows(top, total, target)
    for j in range(1, NX):
        send(stat_x.at[0], stat_x.at[j], stat_sem, j - 1, at_x(j))
    for j in range(1, NX):
        arrive(stat_x.at[j], stat_sem, j - 1)
    stat_y[0] = stat_rows(*merge(stat_x, NX))
    for j in range(1, NY):
        send(stat_y.at[0], stat_y.at[j], stat_sem, 2 + j, at_y(j))
    for j in range(1, NY):
        arrive(stat_y.at[j], stat_sem, 2 + j)
    top, total, target = merge(stat_y, NY)
    lse = top + jnp.log(total)
    lossrow[...] = jnp.broadcast_to(lse - target, lossrow.shape)

    def pull(k, carry):
        begin = pl.multiple_of(k * step, step)
        probs = jnp.exp(acc_t[pl.ds(begin, step), :] - lse)
        hit = jnp.where(chunk_ids == ids - begin, 1.0, 0.0)
        up[pl.ds(begin, step), :] = (weight_row * (probs - hit)).astype(BF16)
        return carry

    lax.fori_loop(0, voc_dev // step, pull, 0)

    def block_rows(way, yb):
        block = yb * NX + lax.rem(x + way, NX)
        return pl.ds(pl.multiple_of(block * cols, cols), cols)

    def head_part(way, yb):
        out = jnp.dot(table[block_rows(way, yb), :], up[...], preferred_element_type=F32)
        return [out[:, h * rows : (h + 1) * rows] for h in range(heads)]

    def norm_parts(h, blocks):
        lines = [w[h, block_rows(way, yb), :] for way, yb in blocks]
        out = jnp.dot(jnp.concatenate(lines, axis=0), low[h], preferred_element_type=F32)
        return [out[k * cols : (k + 1) * cols] for k in range(len(blocks))]

    def across_of(n):
        way, b = lax.rem(n, 2), lax.div(n, 2)
        return way, 2 * way + b, 2 * way + b

    def near_of(n):
        way, b = lax.rem(n, 2), lax.div(n, 2)
        yb = 2 - 2 * way + b
        return way, yb, 4 + 4 * way + yb

    def last_of(n):
        way, b = lax.rem(n, 2), lax.div(n, 2)
        yb = 2 * way + b
        return way, yb, 4 + 4 * way + yb

    def loop4(body):
        def run(n, carry):
            body(n)
            return carry

        lax.fori_loop(0, 4, run, 0)

    def x_copy(i, way, slot):
        return pltpu.make_async_remote_copy(
            src_ref=rs_send.at[i, slot], dst_ref=rs_in.at[i, slot],
            send_sem=rs_sem.at[i, 0, slot], recv_sem=rs_sem.at[i, 1, slot],
            device_id=at_x(1 + 2 * way), device_id_type=MESH,
        )

    def x_arrive(i, slot):
        x_copy(i, 0, slot).wait_recv()

    def y_copy(i, yb):
        return pltpu.make_async_remote_copy(
            src_ref=ys_send.at[i, yb], dst_ref=ys_recv.at[i, y],
            send_sem=rs_sem.at[i, 0, 12 + yb], recv_sem=rs_sem.at[i, 1, 12 + y],
            device_id=(seq, yb * NX + x), device_id_type=MESH,
        )

    def y_arrive(i, yb):
        pltpu.make_async_remote_copy(
            src_ref=ys_send.at[i, yb], dst_ref=ys_recv.at[i, yb],
            send_sem=rs_sem.at[i, 0, 12 + yb], recv_sem=rs_sem.at[i, 1, 12 + yb],
            device_id=(seq, yb * NX + x), device_id_type=MESH,
        ).wait_recv()

    def column(i):
        for k in range(2):
            for yb in (k, k + 2):
                x_arrive(i, 4 + yb)
                x_arrive(i, 8 + yb)
                total = rs_own[i, yb] + rs_in[i, 4 + yb].astype(F32) + rs_in[i, 8 + yb].astype(F32)
                rs_own[i, yb] = total
                ys_send[i, yb] = total.astype(BF16)

                @pl.when(y != yb)
                def _():
                    y_copy(i, yb).start()

    def finish(i):
        total = rs_own[i, y]
        for j in range(1, NY):
            peer = lax.rem(y + j, NY)
            y_arrive(i, peer)
            total = total + ys_recv[i, peer].astype(F32)
        return total

    def across_heads(n):
        way, yb, slot = across_of(n)
        for h, part in enumerate(head_part(2, yb)):
            rs_send[h, slot] = part.astype(BF16)
        x_copy(0, way, slot).start()

    def near_heads(n):
        way, yb, slot = near_of(n)
        for h, part in enumerate(head_part(1 + 2 * way, yb)):
            rs_send[h, slot] = part.astype(BF16)
        x_copy(0, way, slot).start()

    def last_heads(n):
        way, yb, slot = last_of(n)
        for h, part in enumerate(head_part(1 + 2 * way, yb)):
            rs_part[h, yb] = part

    def own_heads(n):
        for h, part in enumerate(head_part(0, n)):
            rs_own[h, n] = part

    def send_heads(h):
        def across(n):
            way, yb, slot = across_of(n)
            x_copy(h, way, slot).start()

        def near(n):
            way, yb, slot = near_of(n)
            x_copy(h, way, slot).start()

        loop4(across)
        loop4(near)

    def pass_heads(h):
        def body(n):
            way, yb, slot = last_of(n)
            x_arrive(h, yb)
            rs_send[h, slot] = (rs_part[h, yb] + rs_in[h, yb].astype(F32)).astype(BF16)
            x_copy(h, way, slot).start()

        loop4(body)

    def head_done(h):
        total = finish(h)
        low[h] = total.astype(BF16)
        head_grad[h] = total

    def norm_begin(h):
        i = heads + h
        for stage, shift in (((0, 0, 0), (1, 2, 2), (0, 1, 1), (1, 3, 3)), 1), (
            ((0, 2, 6), (1, 0, 8), (0, 3, 7), (1, 1, 9)), 0
        ):
            blocks = [(2 if shift else 1 + 2 * way, yb) for way, yb, slot in stage]
            for (way, yb, slot), part in zip(stage, norm_parts(h, blocks)):
                rs_send[i, slot] = part.astype(BF16)
                x_copy(i, way, slot).start()

    def norm_pass(h):
        i = heads + h
        stage = ((0, 0, 4), (1, 2, 10), (0, 1, 5), (1, 3, 11))
        for (way, yb, slot), part in zip(stage, norm_parts(h, [(1 + 2 * way, yb) for way, yb, slot in stage])):
            x_arrive(i, yb)
            rs_send[i, slot] = (part + rs_in[i, yb].astype(F32)).astype(BF16)
            x_copy(i, way, slot).start()
        for n, part in enumerate(norm_parts(h, [(0, n) for n in range(4)])):
            rs_own[i, n] = part

    def norm_done(h):
        norm_grad[h] = finish(heads + h)

    def gain_done(h):
        weighed = norm_grad[h] * x_t[...] * r_line[0:1, :]
        part = jnp.sum(weighed.T, axis=0, keepdims=True)
        gain_rows[8 * h : 8 * h + 8, :] = jnp.broadcast_to(part, (8, cols))

    def left_x(i):
        for slot in range(12):
            x_copy(i, 0, slot).wait_send()

    def left_y(i):
        for j in range(1, NY):
            y_copy(i, lax.rem(y + j, NY)).wait_send()

    loop4(across_heads)
    loop4(near_heads)
    loop4(last_heads)
    pass_heads(0)
    send_heads(1)
    loop4(own_heads)
    column(0)
    pass_heads(1)
    head_done(0)
    norm_begin(0)
    column(1)
    norm_pass(0)
    for copy in pending:
        copy.wait_send()
    pending.clear()
    left_x(0)
    left_y(0)
    left_x(1)
    head_done(1)
    norm_begin(1)
    column(2)
    norm_pass(1)
    left_y(1)
    left_x(2)
    norm_done(0)
    gain_done(0)
    column(3)
    norm_done(1)

    for h in range(1, heads):
        gain_done(h)
    line = lax.broadcasted_iota(jnp.int32, (8, cols), 0)
    packed = jnp.where(line == heads, lossrow[...], 0.0)
    for h in range(heads):
        packed = packed + jnp.where(line == h, gain_rows[8 * h : 8 * h + 8, :], 0.0)
    gain_p[0] = packed
    for k in (2, 3, 1):
        send(gain_p.at[0], gain_p.at[k], gain_sem, k - 1, at_pair(k))
    scaled = jnp.zeros((cols, rows), F32)
    for h in range(heads):
        scaled = scaled + gain_cols[h] * norm_grad[h]
    dots = jnp.sum(scaled * x_t[...], axis=0, keepdims=True)
    dot_x[0] = jnp.broadcast_to(dots, (8, rows))
    for j in range(1, NX):
        send(dot_x.at[0], dot_x.at[j], dot_sem, j - 1, at_x(j))
    for j in range(1, NX):
        arrive(dot_x.at[j], dot_sem, j - 1)
    dot_y[0] = dot_x[0] + dot_x[1] + dot_x[2] + dot_x[3]
    for j in range(1, NY):
        send(dot_y.at[0], dot_y.at[j], dot_sem, 2 + j, at_y(j))
    r_row = r_line[0:1, :]
    direct = (head_grad[0] + head_grad[1] + r_row * scaled).T
    for k in range(1, 4):
        arrive(gain_p.at[k], gain_sem, k - 1)
    gain_z[0] = gain_p[0] + gain_p[1] + gain_p[2] + gain_p[3]
    for j in range(1, NZ):
        send(gain_z.at[0], gain_z.at[j], gain_sem, 2 + j, at_z(j))
    for j in range(1, NY):
        arrive(dot_y.at[j], dot_sem, 2 + j)
    dots = dot_y[0] + dot_y[1] + dot_y[2] + dot_y[3]
    back = r_row * r_row * r_row * dots[0:1, :] / width
    back_col = jnp.broadcast_to(back, (rows, rows)).T[:, 0:1]
    grad_out[...] = direct - xg[voc, 0:rows, :].astype(F32) * back_col
    sums = gain_z[0]
    for j in range(1, NZ):
        arrive(gain_z.at[j], gain_sem, 2 + j)
        sums = sums + gain_z[j]
    gain_out[...] = sums[0:heads, :]
    spot = lax.broadcasted_iota(jnp.int32, loss_out.shape, 1)
    losses = jnp.zeros(loss_out.shape, F32)
    tokens = rows * NZ * PER_Z
    for h in range(heads):
        loss = jnp.sum(sums[heads : heads + 1, h * rows : (h + 1) * rows], axis=-1, keepdims=True)
        losses = losses + jnp.where(spot == h, loss / tokens, 0.0)
    loss_out[...] = losses
    for copy in pending:
        copy.wait_send()
    left_y(2)
    left_x(3)
    left_y(3)


def per_device(hidden, head_weight, gains, unembed, targets, loss_weights):
    rows, cols = hidden.shape
    heads = gains.shape[0]
    voc_dev = unembed.shape[1]
    both = heads * rows
    runs = 2 * heads
    vmem = pl.BlockSpec(memory_space=pltpu.VMEM)
    dma = pltpu.SemaphoreType.DMA
    grad, gain, loss = pl.pallas_call(
        kernel,
        out_shape=(
            pltpu.VMEM((rows, cols), F32),
            pltpu.VMEM((heads, cols), F32),
            pltpu.VMEM((8, 128), F32),
        ),
        in_specs=[pl.BlockSpec(memory_space=pltpu.HBM)] * 6,
        out_specs=(vmem, vmem, vmem),
        scratch_shapes=[
            pltpu.VMEM(head_weight.shape, BF16),
            pltpu.VMEM(gains.shape, BF16),
            pltpu.VMEM(targets.shape, jnp.int32),
            pltpu.SMEM(loss_weights.shape, F32),
            pltpu.VMEM((NV, rows + 8 * heads, cols), BF16),
            pltpu.VMEM((NV, both, cols), BF16),
            pltpu.VMEM((heads, rows, NV * cols), BF16),
            pltpu.VMEM((NV * cols, voc_dev), BF16),
            pltpu.VMEM((2, rows // 2, voc_dev), BF16),
            pltpu.VMEM((both, voc_dev), F32),
            pltpu.VMEM((voc_dev, both), F32),
            pltpu.VMEM((voc_dev, both), BF16),
            pltpu.VMEM((heads, cols, rows), BF16),
            pltpu.VMEM((cols, rows), F32),
            pltpu.VMEM((heads, cols, rows), F32),
            pltpu.VMEM((rows, rows), F32),
            pltpu.VMEM((8, rows), F32),
            pltpu.VMEM((8, both), F32),
            pltpu.VMEM((8 * heads, cols), F32),
            pltpu.VMEM((NX, 8, both), F32),
            pltpu.VMEM((NY, 8, both), F32),
            pltpu.VMEM((NX, 8, rows), F32),
            pltpu.VMEM((NY, 8, rows), F32),
            pltpu.VMEM((4, 8, cols), F32),
            pltpu.VMEM((NZ, 8, cols), F32),
            pltpu.VMEM((runs, 12, cols, rows), BF16),
            pltpu.VMEM((runs, 12, cols, rows), BF16),
            pltpu.VMEM((heads, 4, cols, rows), F32),
            pltpu.VMEM((runs, 4, cols, rows), F32),
            pltpu.VMEM((runs, 4, cols, rows), BF16),
            pltpu.VMEM((runs, 4, cols, rows), BF16),
            pltpu.VMEM((heads, cols, rows), F32),
            pltpu.VMEM((heads, cols, rows), F32),
            dma((6,)),
            dma((2, 30)),
            dma((2, 30)),
            dma((2, 4)),
            dma((2, 28)),
            dma((2, 16)),
            dma((2, 6)),
            dma((2, 6)),
            dma((2, 10)),
            dma((runs, 2, 16)),
        ],
        compiler_params=pltpu.CompilerParams(
            collective_id=0, has_side_effects=True, vmem_limit_bytes=60 * 1024 * 1024
        ),
    )(hidden, head_weight, gains, unembed, targets, loss_weights)
    return loss[0, :heads], grad, gain


def solution(mesh):
    in_specs = (
        P("seq", "vocab"),
        P(None, None, "vocab"),
        P(None, "vocab"),
        P("seq", "vocab"),
        P(None, "seq"),
        P(),
    )
    out_specs = (P(), P("seq", "vocab"), P(None, "vocab"))
    return jax.shard_map(
        per_device, mesh=mesh, in_specs=in_specs, out_specs=out_specs, check_vma=False
    )
```

```python
import jax
import jax.numpy as jnp
from jax import lax
from jax.experimental import pallas as pl
from jax.experimental.pallas import tpu as pltpu
from jax.sharding import PartitionSpec as P

eps = 1e-05
NX, NY, NZ, NFAR, NCORE = 4, 4, 8, 2, 2
NV = NX * NY
PER_Z = NFAR * NCORE
MESH = pl.DeviceIdType.MESH
F32, BF16 = jnp.float32, jnp.bfloat16


def kernel(
    hidden_hbm, w_hbm, gains_hbm, unembed_hbm, targets_hbm, weights_hbm,
    grad_out, gain_out, loss_out,
    w, gains, targets, weights, xg, hf, normed, table, relay, acc, acc_t, up, low,
    x_t, gain_cols, rcol, r_line, lossrow, gain_rows,
    stat_x, stat_y, dot_x, dot_y, gain_p, gain_z,
    rs_send, rs_in, rs_part, rs_own, ys_send, ys_recv, head_grad, norm_grad,
    local_sem, xg_sem, hf_sem, far_sem, ring_sem, share_sem, stat_sem, dot_sem, gain_sem, rs_sem,
):
    rows, cols = hidden_hbm.shape
    heads = gains.shape[0]
    both = heads * rows
    voc_dev = unembed_hbm.shape[1]
    width = cols * NV
    seq, voc = lax.axis_index("seq"), lax.axis_index("vocab")
    x, y = lax.rem(voc, NX), lax.div(voc, NX)
    z, far, core = lax.div(seq, PER_Z), lax.rem(lax.div(seq, NCORE), NFAR), lax.rem(seq, NCORE)
    right, left, over = lax.rem(x + 1, NX), lax.rem(x + 3, NX), lax.rem(x + 2, NX)
    levels = NFAR * NY
    level = far * NY + y

    def at_x(j):
        return (seq, y * NX + lax.rem(x + j, NX))

    def at_y(j):
        return (seq, lax.rem(y + j, NY) * NX + x)

    def at_z(j):
        return (lax.rem(z + j, NZ) * PER_Z + far * NCORE + core, voc)

    def at_pair(k):
        other_far = 1 - far if k // 2 else far
        other_core = 1 - core if k % 2 else core
        return (z * PER_Z + other_far * NCORE + other_core, voc)

    def at_level(j):
        other = lax.rem(level + j + levels, levels)
        return (z * PER_Z + lax.div(other, NY) * NCORE + core, lax.rem(other, NY) * NX + x)

    pending = []

    def send(src, dst, sems, k, to):
        copy = pltpu.make_async_remote_copy(
            src_ref=src, dst_ref=dst, send_sem=sems.at[0, k], recv_sem=sems.at[1, k],
            device_id=to, device_id_type=MESH,
        )
        copy.start()
        pending.append(copy)

    def arrive(dst, sems, k):
        pltpu.make_async_remote_copy(
            src_ref=dst, dst_ref=dst, send_sem=sems.at[0, k], recv_sem=sems.at[1, k],
            device_id=at_x(1), device_id_type=MESH,
        ).wait_recv()

    own_rows = pl.ds(pl.multiple_of(seq * rows, rows), rows)
    fetches = [
        pltpu.make_async_copy(hidden_hbm, xg.at[voc, pl.ds(0, rows), :], local_sem.at[0]),
        pltpu.make_async_copy(unembed_hbm, table.at[own_rows, :], local_sem.at[1]),
        pltpu.make_async_copy(gains_hbm, gains, local_sem.at[2]),
        pltpu.make_async_copy(targets_hbm, targets, local_sem.at[3]),
        pltpu.make_async_copy(weights_hbm, weights, local_sem.at[4]),
        pltpu.make_async_copy(w_hbm, w, local_sem.at[5]),
    ]
    for fetch in fetches:
        fetch.start()
    barrier = pltpu.get_barrier_semaphore()
    partners = (
        [at_x(j) for j in range(1, NX)] + [at_y(j) for j in range(1, NY)]
        + [at_z(j) for j in range(1, NZ)] + [at_pair(k) for k in range(1, 4)]
        + [at_level(2), at_level(-2)]
    )
    for partner in partners:
        pl.semaphore_signal(barrier, inc=1, device_id=partner, device_id_type=MESH)
    for k in range(5):
        fetches[k].wait()
    gain_lines = gains[...].astype(F32)
    gain_pad = jnp.concatenate(
        [jnp.broadcast_to(gain_lines[h : h + 1], (8, cols)) for h in range(heads)], axis=0
    )
    xg[voc, rows : rows + 8 * heads, :] = gain_pad.astype(BF16)
    pl.semaphore_wait(barrier, len(partners))

    def row(q):
        return lax.rem(y + NY - q, NY) * NX

    def gather_begin(at, sems, base):
        for j in range(1, NY):
            send(at(voc), at(voc), sems, base + j - 1, at_y(j))
        send(at(voc), at(voc), sems, base + 3, at_x(1))
        send(at(voc), at(voc), sems, base + 7, at_x(NX - 1))

    def gather_row(at, sems, base, q):
        slot = row(q) + x
        arrive(at(slot), sems, base + q - 1)
        send(at(slot), at(slot), sems, base + 3 + q, at_x(1))
        send(at(slot), at(slot), sems, base + 7 + q, at_x(NX - 1))

    def gather_cross(at, sems, base, q):
        if q < 2:
            slot, k, to = row(q) + left, 3 + q, at_x(1)
        else:
            slot, k, to = row(q) + right, 7 + q, at_x(NX - 1)
        arrive(at(slot), sems, base + k)
        send(at(slot), at(slot), sems, base + 11 + q, to)

    def gather_near(at, sems, base):
        for q in (2, 3):
            arrive(at(row(q) + left), sems, base + 3 + q)
        for q in (0, 1):
            arrive(at(row(q) + right), sems, base + 7 + q)

    def gather_over(at, sems, base):
        for q in range(NY):
            arrive(at(row(q) + over), sems, base + 11 + q)

    def gather_end(at, sems, base):
        gather_near(at, sems, base)
        gather_over(at, sems, base)

    half = rows // 2
    pads = 8 * heads

    def x_at(t):
        return lambda slot: xg.at[slot, pl.ds(t * half, half + t * pads), :]

    def hf_at(t):
        return lambda slot: hf.at[slot, pl.ds(t * rows, rows), :]

    def slab(zz, e, own=True, first=0, count=rows):
        far_e = 1 - far if e else far
        core_e = core if own else 1 - core
        start = pl.multiple_of((zz * PER_Z + far_e * NCORE + core_e) * rows + first, count)
        return table.at[pl.ds(start, count), :]

    def z_at(j):
        return lax.rem(z + j + NZ, NZ)

    def share(e, k, zz):
        send(slab(zz, e), slab(zz, e), share_sem, e * NZ + k, at_pair(1))

    def part_of(zz, e, p):
        return slab(zz, e, True, p * half, half)

    leg = 2 - 4 * core

    def far_begin(p):
        send(part_of(z, 0, p), relay.at[p], far_sem, p, at_level(leg))

    def far_pass(p):
        arrive(relay.at[p], far_sem, p)
        source = lax.rem(level - leg + levels, levels)
        begin = (z * PER_Z + lax.div(source, NY) * NCORE + core) * rows + p * half
        place = table.at[pl.ds(pl.multiple_of(begin, half), half), :]
        send(relay.at[p], place, far_sem, 2 + p, at_level(leg))

    def ring_send(zz, e, way, h, p):
        block = part_of(zz, e, p)
        send(block, block, ring_sem, e * 14 + way * 7 + (h - 1) * 2 + (p if h < 4 else 0),
             at_z(NZ - 1 if way else 1))

    def ring_arrive(zz, e, way, h, p):
        arrive(part_of(zz, e, p), ring_sem, e * 14 + way * 7 + (h - 1) * 2 + (p if h < 4 else 0))

    def ring_begin(e, turn):
        if e:
            arrive(part_of(z, 1, turn), far_sem, 2 + turn)
        for way in range(2):
            ring_send(z, e, way, 1, turn if e else way ^ turn)
        if turn:
            share(e, 0, z)

    def ring_step(e, h, turn):
        for way in range(2):
            p = turn if e and h == 1 else way ^ turn
            zz = z_at(h if way else -h)
            ring_arrive(zz, e, way, h, p)
            if h < 3 or p == way:
                ring_send(zz, e, way, h + 1, p)
            if turn:
                share(e, 2 * h - 1 + way, zz)

    def ring_end(e):
        zz = z_at(4)
        for way in range(2):
            ring_arrive(zz, e, way, 4, way)
        share(e, 7, zz)

    def logit_blocks(blocks):
        left_parts, right_parts = [], []
        for block in blocks:
            lines = [
                hf[block, t * rows + h * half : t * rows + (h + 1) * half, :]
                for h in range(heads) for t in range(2)
            ]
            left_parts.append(jnp.concatenate(lines, axis=0))
            right_parts.append(table[pl.ds(pl.multiple_of(block * cols, cols), cols), :])
        return jnp.dot(
            jnp.concatenate(left_parts, axis=1), jnp.concatenate(right_parts, axis=0),
            preferred_element_type=F32,
        )

    def slab_at(k):
        return z_at((k + 1) // 2 * (1 - 2 * (k % 2)))

    def consume(slabs):
        blocks = []
        for k in slabs:
            zz = slab_at(k)
            arrive(slab(zz, 1, False), share_sem, NZ + k)
            blocks.append(zz * NFAR + 1 - far)
        acc[...] += logit_blocks(blocks)

    for k, t in enumerate((1, 0)):
        gather_begin(x_at(t), xg_sem, 15 * t)
        ring_begin(0, k)
        far_begin(k)

    own_x = xg[voc, 0:rows, :].astype(F32)
    x_t[...] = own_x.T
    for h in range(heads):
        gain_cols[h] = jnp.broadcast_to(gain_lines[h : h + 1], (rows, cols)).T

    def project(t, between):
        lo = t * half

        def square(k, total):
            block = xg[k, lo : lo + half, :].astype(F32)
            return total + block * block

        squares = lax.fori_loop(0, NV, square, jnp.zeros((half, cols), F32))
        r = lax.rsqrt(jnp.sum(squares, axis=-1, keepdims=True) / width + eps)
        rcol[lo : lo + half, :] = jnp.broadcast_to(r, (half, rows))

        def norm(k, carry):
            scaled = xg[k, lo : lo + half, :].astype(F32) * rcol[lo : lo + half, 0:1]
            begin = pl.multiple_of(k * cols, cols)
            gain_k = xg[k, rows : rows + pads, :].astype(F32)
            for h in range(heads):
                line = (scaled * gain_k[8 * h : 8 * h + 1]).astype(BF16)
                normed[h, lo : lo + half, pl.ds(begin, cols)] = line
            return carry

        between(0)
        lax.fori_loop(0, NV, norm, 0)
        for h in range(heads):
            between(1 + h)
            branch = jnp.dot(normed[h, lo : lo + half, :], w[h], preferred_element_type=F32)
            total = xg[voc, lo : lo + half, :].astype(F32) + branch
            at = t * rows + h * half
            hf[voc, at : at + half, :] = total.astype(BF16)
        gather_begin(hf_at(t), hf_sem, 15 * t)

    def rows_of(at, sems, base):
        for q in range(1, NY):
            gather_row(at, sems, base, q)

    def cross_of(at, sems, base):
        for q in (0, 2, 1, 3):
            gather_cross(at, sems, base, q)

    def first_between(k):
        if k == 1:
            ring_step(0, 3, 0)

    def second_between(k):
        if k == 0:
            ring_step(0, 3, 1)
        if k == 1:
            ring_step(1, 1, 0)
        if k == 2:
            rows_of(hf_at(1), hf_sem, 15)

    rows_of(x_at(1), xg_sem, 15)
    ring_step(0, 1, 0)
    far_pass(0)
    rows_of(x_at(0), xg_sem, 0)
    cross_of(x_at(1), xg_sem, 15)
    ring_step(0, 1, 1)
    far_pass(1)
    ring_step(0, 2, 0)
    cross_of(x_at(0), xg_sem, 0)
    ring_begin(1, 0)
    gather_end(x_at(1), xg_sem, 15)
    ring_step(0, 2, 1)
    ring_begin(1, 1)
    fetches[5].wait()
    project(1, first_between)
    gather_end(x_at(0), xg_sem, 0)
    project(0, second_between)
    ring_step(1, 1, 1)
    r_line[...] = rcol[...].T[0:8, :]
    ring_end(0)
    cross_of(hf_at(1), hf_sem, 15)
    ring_step(1, 2, 0)
    rows_of(hf_at(0), hf_sem, 0)
    ring_step(1, 2, 1)
    cross_of(hf_at(0), hf_sem, 0)
    ring_step(1, 3, 0)
    gather_near(hf_at(1), hf_sem, 15)
    gather_near(hf_at(0), hf_sem, 0)

    for k in range(NZ):
        arrive(slab(slab_at(k), 0, False), share_sem, k)
    column_1 = lax.rem(x + NX - lax.rem(x + far, 2), NX)
    column_2 = lax.rem(column_1 + 2, NX)
    acc[...] = logit_blocks([yb * NX + column_1 for yb in range(NY)])
    ring_step(1, 3, 1)
    gather_over(hf_at(1), hf_sem, 15)
    gather_over(hf_at(0), hf_sem, 0)
    acc[...] += logit_blocks([yb * NX + column_2 for yb in range(NY)])
    consume((0, 1, 2))
    consume((3, 4, 5, 6))
    ring_end(1)
    consume((7,))

    step = 128
    ids = jnp.concatenate([targets[h : h + 1, :] for h in range(heads)], axis=1) - voc * voc_dev
    chunk_ids = lax.broadcasted_iota(jnp.int32, (step, both), 0)
    lane = lax.broadcasted_iota(jnp.int32, (1, both), 1)
    weight_row = jnp.full((1, both), weights[0], F32)
    for h in range(1, heads):
        weight_row = jnp.where(lane >= h * rows, weights[h], weight_row)

    def stat_rows(top, total, target):
        line = lax.broadcasted_iota(jnp.int32, (8, both), 0)
        return jnp.where(line == 0, top, jnp.where(line == 1, total, jnp.where(line == 2, target, 0.0)))

    def merge(slots, count):
        tops = [slots[j, 0:1, :] for j in range(count)]
        top = tops[0]
        for other in tops[1:]:
            top = jnp.maximum(top, other)
        total = jnp.zeros_like(top)
        target = jnp.zeros_like(top)
        for j in range(count):
            total = total + slots[j, 1:2, :] * jnp.exp(tops[j] - top)
            target = target + slots[j, 2:3, :]
        return top, total, target

    def turn(k, top):
        begin = pl.multiple_of(k * step, step)
        chunk = acc[:, pl.ds(begin, step)].T
        acc_t[pl.ds(begin, step), :] = chunk
        return jnp.maximum(top, jnp.max(chunk, axis=0, keepdims=True))

    first_chunk = acc[:, 0:step].T
    acc_t[0:step, :] = first_chunk
    top = lax.fori_loop(1, voc_dev // step, turn, jnp.max(first_chunk, axis=0, keepdims=True))

    def gauge(k, sums):
        begin = pl.multiple_of(k * step, step)
        chunk = acc_t[pl.ds(begin, step), :]
        total = jnp.sum(jnp.exp(chunk - top), axis=0, keepdims=True)
        hit = jnp.where(chunk_ids == ids - begin, chunk, 0.0)
        return sums[0] + total, sums[1] + jnp.sum(hit, axis=0, keepdims=True)

    empty = jnp.zeros((1, both), F32)
    total, target = lax.fori_loop(0, voc_dev // step, gauge, (empty, empty))
    stat_x[0] = stat_rows(top, total, target)
    for j in range(1, NX):
        send(stat_x.at[0], stat_x.at[j], stat_sem, j - 1, at_x(j))
    for j in range(1, NX):
        arrive(stat_x.at[j], stat_sem, j - 1)
    stat_y[0] = stat_rows(*merge(stat_x, NX))
    for j in range(1, NY):
        send(stat_y.at[0], stat_y.at[j], stat_sem, 2 + j, at_y(j))
    for j in range(1, NY):
        arrive(stat_y.at[j], stat_sem, 2 + j)
    top, total, target = merge(stat_y, NY)
    lse = top + jnp.log(total)
    lossrow[...] = jnp.broadcast_to(lse - target, lossrow.shape)

    def pull(k, carry):
        begin = pl.multiple_of(k * step, step)
        probs = jnp.exp(acc_t[pl.ds(begin, step), :] - lse)
        hit = jnp.where(chunk_ids == ids - begin, 1.0, 0.0)
        up[pl.ds(begin, step), :] = (weight_row * (probs - hit)).astype(BF16)
        return carry

    lax.fori_loop(0, voc_dev // step, pull, 0)

    def block_rows(way, yb):
        block = yb * NX + lax.rem(x + way, NX)
        return pl.ds(pl.multiple_of(block * cols, cols), cols)

    def head_parts(blocks):
        lines = [table[block_rows(way, yb), :] for way, yb in blocks]
        out = jnp.dot(jnp.concatenate(lines, axis=0), up[...], preferred_element_type=F32)
        return [
            [out[k * cols : (k + 1) * cols, h * rows : (h + 1) * rows] for h in range(heads)]
            for k in range(len(blocks))
        ]

    def norm_parts(h, blocks):
        lines = [w[h, block_rows(way, yb), :] for way, yb in blocks]
        out = jnp.dot(jnp.concatenate(lines, axis=0), low[h], preferred_element_type=F32)
        return [out[k * cols : (k + 1) * cols] for k in range(len(blocks))]

    def across_of(n):
        way, b = lax.rem(n, 2), lax.div(n, 2)
        return way, 2 * way + b, 2 * way + b

    def near_of(n):
        way, b = lax.rem(n, 2), lax.div(n, 2)
        yb = 2 - 2 * way + b
        return way, yb, 4 + 4 * way + yb

    def last_of(n):
        way, b = lax.rem(n, 2), lax.div(n, 2)
        yb = 2 * way + b
        return way, yb, 4 + 4 * way + yb

    def loop4(body):
        def run(n, carry):
            body(n)
            return carry

        lax.fori_loop(0, 4, run, 0)

    def x_copy(i, way, slot):
        return pltpu.make_async_remote_copy(
            src_ref=rs_send.at[i, slot], dst_ref=rs_in.at[i, slot],
            send_sem=rs_sem.at[i, 0, slot], recv_sem=rs_sem.at[i, 1, slot],
            device_id=at_x(1 + 2 * way), device_id_type=MESH,
        )

    def x_arrive(i, slot):
        x_copy(i, 0, slot).wait_recv()

    def y_copy(i, yb):
        return pltpu.make_async_remote_copy(
            src_ref=ys_send.at[i, yb], dst_ref=ys_recv.at[i, y],
            send_sem=rs_sem.at[i, 0, 12 + yb], recv_sem=rs_sem.at[i, 1, 12 + y],
            device_id=(seq, yb * NX + x), device_id_type=MESH,
        )

    def y_arrive(i, yb):
        pltpu.make_async_remote_copy(
            src_ref=ys_send.at[i, yb], dst_ref=ys_recv.at[i, yb],
            send_sem=rs_sem.at[i, 0, 12 + yb], recv_sem=rs_sem.at[i, 1, 12 + yb],
            device_id=(seq, yb * NX + x), device_id_type=MESH,
        ).wait_recv()

    def column(i):
        for k in range(2):
            for yb in (k, k + 2):
                x_arrive(i, 4 + yb)
                x_arrive(i, 8 + yb)
                total = rs_own[i, yb] + rs_in[i, 4 + yb].astype(F32) + rs_in[i, 8 + yb].astype(F32)
                rs_own[i, yb] = total
                ys_send[i, yb] = total.astype(BF16)

                @pl.when(y != yb)
                def _():
                    y_copy(i, yb).start()

    def finish(i):
        total = rs_own[i, y]
        for j in range(1, NY):
            peer = lax.rem(y + j, NY)
            y_arrive(i, peer)
            total = total + ys_recv[i, peer].astype(F32)
        return total

    def begin_heads(stage):
        parts = head_parts([(step, yb) for step, way, yb, slot in stage])
        for (step, way, yb, slot), part in zip(stage, parts):
            for h in range(heads):
                rs_send[h, slot] = part[h].astype(BF16)
            x_copy(0, way, slot).start()

    def last_heads():
        stage = ((0, 0, 4), (1, 2, 10), (0, 1, 5), (1, 3, 11))
        parts = head_parts([(1 + 2 * way, yb) for way, yb, slot in stage])
        for (way, yb, slot), part in zip(stage, parts):
            for h in range(1, heads):
                rs_part[h, yb] = part[h]
            x_arrive(0, yb)
            rs_send[0, slot] = (part[0] + rs_in[0, yb].astype(F32)).astype(BF16)
            x_copy(0, way, slot).start()

    def own_heads():
        for n, part in enumerate(head_parts([(0, n) for n in range(4)])):
            for h in range(heads):
                rs_own[h, n] = part[h]

    def send_heads(h):
        def across(n):
            way, yb, slot = across_of(n)
            x_copy(h, way, slot).start()

        def near(n):
            way, yb, slot = near_of(n)
            x_copy(h, way, slot).start()

        loop4(across)
        loop4(near)

    def pass_heads(h):
        def body(n):
            way, yb, slot = last_of(n)
            x_arrive(h, yb)
            rs_send[h, slot] = (rs_part[h, yb] + rs_in[h, yb].astype(F32)).astype(BF16)
            x_copy(h, way, slot).start()

        loop4(body)

    def head_done(h):
        total = finish(h)
        low[h] = total.astype(BF16)
        head_grad[h] = total

    def norm_begin(h):
        i = heads + h
        for stage, shift in (((0, 0, 0), (1, 2, 2), (0, 1, 1), (1, 3, 3)), 1), (
            ((0, 2, 6), (1, 0, 8), (0, 3, 7), (1, 1, 9)), 0
        ):
            blocks = [(2 if shift else 1 + 2 * way, yb) for way, yb, slot in stage]
            for (way, yb, slot), part in zip(stage, norm_parts(h, blocks)):
                rs_send[i, slot] = part.astype(BF16)
                x_copy(i, way, slot).start()

    def norm_pass(h):
        i = heads + h
        stage = ((0, 0, 4), (1, 2, 10), (0, 1, 5), (1, 3, 11))
        for (way, yb, slot), part in zip(stage, norm_parts(h, [(1 + 2 * way, yb) for way, yb, slot in stage])):
            x_arrive(i, yb)
            rs_send[i, slot] = (part + rs_in[i, yb].astype(F32)).astype(BF16)
            x_copy(i, way, slot).start()
        for n, part in enumerate(norm_parts(h, [(0, n) for n in range(4)])):
            rs_own[i, n] = part

    def norm_done(h):
        norm_grad[h] = finish(heads + h)

    def gain_done(h):
        weighed = norm_grad[h] * x_t[...] * r_line[0:1, :]
        part = jnp.sum(weighed.T, axis=0, keepdims=True)
        gain_rows[8 * h : 8 * h + 8, :] = jnp.broadcast_to(part, (8, cols))

    def left_x(i):
        for slot in range(12):
            x_copy(i, 0, slot).wait_send()

    def left_y(i):
        for j in range(1, NY):
            y_copy(i, lax.rem(y + j, NY)).wait_send()

    begin_heads(((2, 0, 0, 0), (2, 1, 2, 2)))
    begin_heads(((2, 0, 1, 1), (2, 1, 3, 3)))
    begin_heads(((1, 0, 2, 6), (3, 1, 0, 8)))
    begin_heads(((1, 0, 3, 7), (3, 1, 1, 9)))
    last_heads()
    send_heads(1)
    own_heads()
    column(0)
    pass_heads(1)
    head_done(0)
    norm_begin(0)
    column(1)
    norm_pass(0)
    for copy in pending:
        copy.wait_send()
    pending.clear()
    left_x(0)
    left_y(0)
    left_x(1)
    head_done(1)
    norm_begin(1)
    column(2)
    norm_pass(1)
    left_y(1)
    left_x(2)
    norm_done(0)
    gain_done(0)
    column(3)
    norm_done(1)

    for h in range(1, heads):
        gain_done(h)
    line = lax.broadcasted_iota(jnp.int32, (8, cols), 0)
    packed = jnp.where(line == heads, lossrow[...], 0.0)
    for h in range(heads):
        packed = packed + jnp.where(line == h, gain_rows[8 * h : 8 * h + 8, :], 0.0)
    gain_p[0] = packed
    for k in (2, 3, 1):
        send(gain_p.at[0], gain_p.at[k], gain_sem, k - 1, at_pair(k))
    scaled = jnp.zeros((cols, rows), F32)
    for h in range(heads):
        scaled = scaled + gain_cols[h] * norm_grad[h]
    dots = jnp.sum(scaled * x_t[...], axis=0, keepdims=True)
    dot_x[0] = jnp.broadcast_to(dots, (8, rows))
    for j in range(1, NX):
        send(dot_x.at[0], dot_x.at[j], dot_sem, j - 1, at_x(j))
    for j in range(1, NX):
        arrive(dot_x.at[j], dot_sem, j - 1)
    dot_y[0] = dot_x[0] + dot_x[1] + dot_x[2] + dot_x[3]
    for j in range(1, NY):
        send(dot_y.at[0], dot_y.at[j], dot_sem, 2 + j, at_y(j))
    r_row = r_line[0:1, :]
    direct = (head_grad[0] + head_grad[1] + r_row * scaled).T
    for k in range(1, 4):
        arrive(gain_p.at[k], gain_sem, k - 1)
    gain_z[0] = gain_p[0] + gain_p[1] + gain_p[2] + gain_p[3]
    for j in range(1, NZ):
        send(gain_z.at[0], gain_z.at[j], gain_sem, 2 + j, at_z(j))
    for j in range(1, NY):
        arrive(dot_y.at[j], dot_sem, 2 + j)
    dots = dot_y[0] + dot_y[1] + dot_y[2] + dot_y[3]
    back = r_row * r_row * r_row * dots[0:1, :] / width
    back_col = jnp.broadcast_to(back, (rows, rows)).T[:, 0:1]
    grad_out[...] = direct - xg[voc, 0:rows, :].astype(F32) * back_col
    sums = gain_z[0]
    for j in range(1, NZ):
        arrive(gain_z.at[j], gain_sem, 2 + j)
        sums = sums + gain_z[j]
    gain_out[...] = sums[0:heads, :]
    spot = lax.broadcasted_iota(jnp.int32, loss_out.shape, 1)
    losses = jnp.zeros(loss_out.shape, F32)
    tokens = rows * NZ * PER_Z
    for h in range(heads):
        loss = jnp.sum(sums[heads : heads + 1, h * rows : (h + 1) * rows], axis=-1, keepdims=True)
        losses = losses + jnp.where(spot == h, loss / tokens, 0.0)
    loss_out[...] = losses
    for copy in pending:
        copy.wait_send()
    left_y(2)
    left_x(3)
    left_y(3)


def per_device(hidden, head_weight, gains, unembed, targets, loss_weights):
    rows, cols = hidden.shape
    heads = gains.shape[0]
    voc_dev = unembed.shape[1]
    both = heads * rows
    runs = 2 * heads
    vmem = pl.BlockSpec(memory_space=pltpu.VMEM)
    dma = pltpu.SemaphoreType.DMA
    grad, gain, loss = pl.pallas_call(
        kernel,
        out_shape=(
            pltpu.VMEM((rows, cols), F32),
            pltpu.VMEM((heads, cols), F32),
            pltpu.VMEM((8, 128), F32),
        ),
        in_specs=[pl.BlockSpec(memory_space=pltpu.HBM)] * 6,
        out_specs=(vmem, vmem, vmem),
        scratch_shapes=[
            pltpu.VMEM(head_weight.shape, BF16),
            pltpu.VMEM(gains.shape, BF16),
            pltpu.VMEM(targets.shape, jnp.int32),
            pltpu.SMEM(loss_weights.shape, F32),
            pltpu.VMEM((NV, rows + 8 * heads, cols), BF16),
            pltpu.VMEM((NV, both, cols), BF16),
            pltpu.VMEM((heads, rows, NV * cols), BF16),
            pltpu.VMEM((NV * cols, voc_dev), BF16),
            pltpu.VMEM((2, rows // 2, voc_dev), BF16),
            pltpu.VMEM((both, voc_dev), F32),
            pltpu.VMEM((voc_dev, both), F32),
            pltpu.VMEM((voc_dev, both), BF16),
            pltpu.VMEM((heads, cols, rows), BF16),
            pltpu.VMEM((cols, rows), F32),
            pltpu.VMEM((heads, cols, rows), F32),
            pltpu.VMEM((rows, rows), F32),
            pltpu.VMEM((8, rows), F32),
            pltpu.VMEM((8, both), F32),
            pltpu.VMEM((8 * heads, cols), F32),
            pltpu.VMEM((NX, 8, both), F32),
            pltpu.VMEM((NY, 8, both), F32),
            pltpu.VMEM((NX, 8, rows), F32),
            pltpu.VMEM((NY, 8, rows), F32),
            pltpu.VMEM((4, 8, cols), F32),
            pltpu.VMEM((NZ, 8, cols), F32),
            pltpu.VMEM((runs, 12, cols, rows), BF16),
            pltpu.VMEM((runs, 12, cols, rows), BF16),
            pltpu.VMEM((heads, 4, cols, rows), F32),
            pltpu.VMEM((runs, 4, cols, rows), F32),
            pltpu.VMEM((runs, 4, cols, rows), BF16),
            pltpu.VMEM((runs, 4, cols, rows), BF16),
            pltpu.VMEM((heads, cols, rows), F32),
            pltpu.VMEM((heads, cols, rows), F32),
            dma((6,)),
            dma((2, 30)),
            dma((2, 30)),
            dma((2, 4)),
            dma((2, 28)),
            dma((2, 16)),
            dma((2, 6)),
            dma((2, 6)),
            dma((2, 10)),
            dma((runs, 2, 16)),
        ],
        compiler_params=pltpu.CompilerParams(
            collective_id=0, has_side_effects=True, vmem_limit_bytes=60 * 1024 * 1024
        ),
    )(hidden, head_weight, gains, unembed, targets, loss_weights)
    return loss[0, :heads], grad, gain


def solution(mesh):
    in_specs = (
        P("seq", "vocab"),
        P(None, None, "vocab"),
        P(None, "vocab"),
        P("seq", "vocab"),
        P(None, "seq"),
        P(),
    )
    out_specs = (P(), P("seq", "vocab"), P(None, "vocab"))
    return jax.shard_map(
        per_device, mesh=mesh, in_specs=in_specs, out_specs=out_specs, check_vma=False
    )
```
